256 devices in a mesh: rows: 64 (over z_hi, x, y, core), cols: 4 (over z_lo).
Axes of the slice: x: 4, y: 4, z: 8 (z_hi: 2, z_lo: 4; z = z_hi * 4 + z_lo), core: 2. Of those that a mesh axis runs over, the one named last changes fastest.
Arguments:
- snapshots: float32 [32768, 4096], P('rows', 'cols'), may hold values from -144 to 144
- partner_slot: int32 [8], replicated, may hold values from 0 to 7, each once
Outputs:
- next_blocks: float32 [32768, 4096], P('rows', 'cols')
- energies: float32 [4096], P('cols')
The draws below stay inside these ranges and needn't reach their ends.
Inputs may be any that keep to these rules, and one draw needn't show every extreme that they name: `partner_slot`: each of the 8 pair numbers appears exactly once.
All inputs are finite; a program needn't handle non-finite values.
Results may differ from the reference program's by a relative error of at most 0.0001.
Values sent between devices are 32-bit elements; how exact they have to be, the bound alone decides.
A program may use at most 64 MiB of HBM per device.

```python
import jax
import jax.numpy as jnp
from jax import lax

BW = 256
SWEEPS = 4
PAIRS = 8
NC = 4096
ROWS = 32768


def draw_snapshots(key, part):
    key = jax.random.fold_in(key, 7)
    row_key, col_key, noise_key, basis_key, mixing_key = jax.random.split(key, 5)
    mode_count = 2 * BW
    position = jnp.arange(ROWS, dtype=jnp.float32) / max(ROWS - 1, 1)
    col_scale = jnp.exp(jax.random.uniform(col_key, (NC,), minval=jnp.log(0.4), maxval=jnp.log(4.0)))
    order = jnp.arange(1, mode_count + 1, dtype=jnp.float32)
    row_scale = jnp.exp(jax.random.uniform(row_key, (ROWS,), minval=jnp.log(0.4), maxval=jnp.log(4.0)))
    noise = jax.random.normal(noise_key, (ROWS, NC))
    spectrum = order ** (-1.0)
    share = 0.8
    spectrum = spectrum / jnp.sum(spectrum)
    basis = jax.random.normal(basis_key, (ROWS, mode_count))
    mixing = jax.random.normal(mixing_key, (mode_count, NC)) * jnp.sqrt(spectrum)[:, None]
    coherent = jnp.dot(basis, mixing, precision=lax.Precision.HIGHEST, preferred_element_type=jnp.float32)
    field = jnp.clip(share * coherent + (1.0 - share * share) ** 0.5 * noise, -6.0, 6.0)
    return ((row_scale * (0.5 + position))[:, None] * col_scale[None, :] * field).astype(jnp.float32)


def setup_inputs(seed: int = 0) -> dict:
    seeds = jax.random.split(jax.random.key(seed), 3)
    snapshots = draw_snapshots(jax.random.fold_in(seeds[2], 71), 0)
    partner_slot = jax.random.permutation(seeds[1], PAIRS).astype(jnp.int32)
    return dict(snapshots=snapshots, partner_slot=partner_slot)


def matmul(left, right):
    return jnp.dot(left, right, precision=lax.Precision.HIGHEST, preferred_element_type=jnp.float32)

def damped_rotation(cross_part, diag_left, diag_right):
    half_width = cross_part.shape[0]
    gap_diag = diag_right[None, :] - diag_left[:, None]
    coupling = cross_part * gap_diag / (gap_diag * gap_diag + 4.0 * cross_part * cross_part + 0.25 * diag_left[:, None] * diag_right[None, :])
    zero_part = jnp.zeros((half_width, half_width), jnp.float32)
    skew = jnp.concatenate([jnp.concatenate([zero_part, coupling], 1), jnp.concatenate([-coupling.T, zero_part], 1)], 0)
    norm_scale = 1.0 / jnp.sqrt(1.0 + 2.0 * jnp.sum(coupling * coupling))
    current = (jnp.eye(2 * half_width, dtype=jnp.float32) + skew) * norm_scale
    for sweep in range(SWEEPS):
        product = matmul(current.T, current)
        current = 1.5 * current - 0.5 * matmul(current, product)
    return current

def reference(snapshots, partner_slot):
    lefts = []
    rights = []
    energy_parts = []
    for pair_index in range(PAIRS):
        pair_block = snapshots[:, pair_index * 2 * BW:(pair_index + 1) * 2 * BW]
        gram_sum = matmul(pair_block.T, pair_block)
        diagonal = jnp.diagonal(gram_sum)
        rotation = damped_rotation(gram_sum[:BW, BW:], diagonal[:BW], diagonal[BW:])
        rotated = matmul(pair_block, rotation)
        energy_parts.append(lax.optimization_barrier(jnp.sum(rotated * rotated, axis=0)) / ROWS)
        lefts.append(rotated[:, :BW])
        rights.append(rotated[:, BW:])
    right_stack = jnp.stack(rights)
    moved = jnp.zeros_like(right_stack).at[partner_slot].set(right_stack)
    pieces = []
    for pair_index in range(PAIRS):
        pieces.append(lefts[pair_index])
        pieces.append(moved[pair_index])
    return (jnp.concatenate(pieces, 1), jnp.concatenate(energy_parts))
```

```python
import functools

import jax
import jax.numpy as jnp
from jax import lax
from jax.experimental import pallas as pl
from jax.experimental.pallas import tpu as pltpu
from jax.sharding import PartitionSpec as P

BW = 256
SWEEPS = 4
MESH = pl.DeviceIdType.MESH
F32 = jnp.float32
BF16 = jnp.bfloat16
XY = 16
CHUNK = 32
LAG = 3


def split(value):
    high = value.astype(BF16)
    return high, (value - high.astype(F32)).astype(BF16)


def dot(left, right, contract=((1,), (0,))):
    return lax.dot_general(left, right, (contract, ((), ())), preferred_element_type=F32)


def dot3(left, right, contract=((1,), (0,))):
    return dot(left[0], right[0], contract) + (
        dot(left[0], right[1], contract) + dot(left[1], right[0], contract)
    )


def coupling_of(cross, diag_tile):
    left_cols = []
    right_rows = []
    for half in range(2):
        left_row = jnp.broadcast_to(diag_tile[half : half + 1, :], (128, 128))
        left_cols.append(jnp.transpose(left_row))
        right_rows.append(diag_tile[2 + half : 3 + half, :])
    left = jnp.concatenate([jnp.concatenate([part, part], 1) for part in left_cols], 0)
    right = jnp.broadcast_to(jnp.concatenate(right_rows, 1), (BW, BW))
    gap = right - left
    return cross * gap / (gap * gap + 4.0 * cross * cross + 0.25 * left * right)


def polynomials(starts, scale):
    eye = (
        lax.broadcasted_iota(jnp.int32, (BW, BW), 0) == lax.broadcasted_iota(jnp.int32, (BW, BW), 1)
    ).astype(F32)
    squares = [(eye + start) * (scale * scale) for start in starts]
    totals = []
    for sweep in range(SWEEPS):
        steps = [1.5 * eye - 0.5 * square for square in squares]
        step_parts = [split(step) for step in steps]
        if sweep == 0:
            totals = [scale * step for step in steps]
        else:
            totals = [dot3(split(total), step) for total, step in zip(totals, step_parts)]
        if sweep < SWEEPS - 1:
            halves = [dot3(split(square), step) for square, step in zip(squares, step_parts)]
            squares = [dot3(split(half), step) for half, step in zip(halves, step_parts)]
    return totals


def pick(options, index):
    value = options[0]
    for position in range(1, len(options)):
        value = jnp.where(index == position, options[position], value)
    return value


def kernel(
    cap, chunks, x_hbm, ps_ref, out_hbm, en_ref,
    own, xh, xl, rh, rl, lefts, rights, fin,
    gmine, gsend, gpeer, rs, zsend, zrecv, ag, rsend, rrecv,
    esend, epeer, exy, ez,
    mid_stage, out_stage, from_outer, from_mid, from_inner,
    load_sem, store_sem, pair_s, pair_r, rs_s, rs_r, z_s, z_r, ag_s, ag_r, ro_s, ro_r,
    e_s, e_r, exy_s, exy_r, in_s, in_r, mid_s, mid_r, out_s, out_r,
):
    row = lax.axis_index("rows")
    z = lax.axis_index("cols")
    core = row % 2
    xy = (row // 2) % XY
    zh = row // (2 * XY)
    side = z // 2
    is_outer = (z % 3) == 0
    is_inner = (z % 3) != 0
    sibling = {"rows": row + 1 - 2 * core}
    far = {"rows": (row + 2 * XY) % (4 * XY)}
    inner_peer = {"cols": 1 + z // 3}
    outer_peer = {"cols": lax.rem(3 * z + 1, 4)}
    mid_peer = {"cols": 3 - z}

    def plane_peer(step):
        return {"rows": zh * 2 * XY + ((xy + step) % XY) * 2 + core}

    def remote(src, dst, send, recv, device):
        return pltpu.make_async_remote_copy(
            src_ref=src, dst_ref=dst, send_sem=send, recv_sem=recv, device_id=device, device_id_type=MESH
        )

    def greet(device):
        pl.semaphore_signal(barrier, inc=1, device_id=device, device_id_type=MESH)

    loads = []
    for pair in range(2):
        load = pltpu.make_async_copy(
            x_hbm.at[:, pl.ds(pair * 2 * BW, 2 * BW)], own.at[pair], load_sem.at[pair]
        )
        load.start()
        loads.append(load)
    barrier = pltpu.get_barrier_semaphore()
    greet(sibling)
    greet(far)

    @pl.loop(1, XY)
    def _(step):
        greet(plane_peer(step))

    @pl.when(is_outer)
    def _():
        greet(inner_peer)

    @pl.when(is_inner)
    def _():
        greet(outer_peer)
        greet(mid_peer)

    for load in loads:
        load.wait()

    def gram(pair, target):
        high, low = split(own[pair])
        xh[pair] = high
        xl[pair] = low
        rows = ((0,), (0,))
        cross = dot3((high[:, :BW], low[:, :BW]), (high[:, BW:], low[:, BW:]), rows)
        target[:, 0:16, :] = cross[:, :128].reshape(XY, 16, 128)
        target[:, 16:32, :] = cross[:, 128:].reshape(XY, 16, 128)
        values = own[pair]
        diagonal = jnp.sum(values * values, axis=0, keepdims=True)
        tile = jnp.concatenate(
            [diagonal[:, 128 * part : 128 * (part + 1)] for part in range(4)]
            + [jnp.zeros((4, 128), F32)],
            0,
        )
        target[:, 32:40, :] = jnp.broadcast_to(tile[None], (XY, 8, 128))

    gram(1 - core, gsend)

    @pl.when(is_outer)
    def _():
        pl.semaphore_wait(barrier, 18)

    @pl.when(is_inner)
    def _():
        pl.semaphore_wait(barrier, 19)

    to_sibling = remote(gsend, gpeer, pair_s, pair_r, sibling)
    to_sibling.start()
    gram(core, gmine)
    to_sibling.wait_recv()
    gmine[...] = gmine[...] + gpeer[...]

    def rs_copy(step):
        target = (xy + step) % XY
        return remote(gmine.at[target], rs.at[xy], rs_s.at[target], rs_r.at[xy], plane_peer(step))

    def rs_arrival(step):
        source = (xy + step) % XY
        return remote(gmine.at[source], rs.at[source], rs_s.at[source], rs_r.at[source], plane_peer(step))

    @pl.loop(1, XY)
    def _(step):
        rs_copy(step).start()

    rs[xy] = gmine[xy]

    @pl.loop(1, XY)
    def _(step):
        rs_arrival(step).wait_recv()

    total = rs[0]
    for chip in range(1, XY):
        total = total + rs[chip]
    zsend[...] = total
    to_far = remote(zsend, zrecv, z_s, z_r, far)
    to_far.start()
    to_far.wait_recv()
    total = zsend[...] + zrecv[...]
    diag_tile = total[32:40, :]
    ag[xy] = total[0:32, :]

    def ag_copy(step):
        return remote(ag.at[xy], ag.at[xy], ag_s.at[step], ag_r.at[xy], plane_peer(step))

    def ag_arrival(step):
        source = (xy + step) % XY
        return remote(ag.at[source], ag.at[source], ag_s.at[step], ag_r.at[source], plane_peer(step))

    @pl.loop(1, XY)
    def _(step):
        ag_copy(step).start()

    @pl.loop(1, XY)
    def _(step):
        ag_arrival(step).wait_recv()

    cross = jnp.concatenate(
        [ag[:, 0:16, :].reshape(BW, 128), ag[:, 16:32, :].reshape(BW, 128)], 1
    )
    coupling = coupling_of(cross, diag_tile)
    scale = lax.rsqrt(jnp.full((1, 1), 1.0, F32) + 2.0 * jnp.sum(coupling * coupling))
    coupling_parts = split(coupling)
    outer_product = dot3(coupling_parts, coupling_parts, ((1,), (1,)))
    inner_product = dot3(coupling_parts, coupling_parts, ((0,), (0,)))
    left_part, right_part = polynomials([outer_product, inner_product], scale)
    rsend[0] = left_part
    rsend[2] = right_part
    rsend[1] = dot3(split(left_part), coupling_parts)
    to_sibling_r = remote(rsend, rrecv, ro_s, ro_r, sibling)
    to_sibling_r.start()

    def spread(pair, source):
        across = source[1]
        for column, row_block, block in (
            (0, 0, source[0]), (1, 0, across), (0, 1, -jnp.transpose(across)), (1, 1, source[2]),
        ):
            high, low = split(block)
            where = (pair, pl.ds(row_block * BW, BW), pl.ds(column * BW, BW))
            rh[where] = high
            rl[where] = low

    rows_here = own.shape[1]
    tile_rows = 128

    def rotate(pair):
        def body(tile, sums):
            rows = pl.ds(pl.multiple_of(tile * tile_rows, tile_rows), tile_rows)
            result = dot3((xh[pair, rows, :], xl[pair, rows, :]), (rh[pair], rl[pair]))
            lefts[pair, rows, :] = result[:, :BW]
            rights[pair, rows, :] = result[:, BW:]
            return sums + jnp.sum(result * result, axis=0, keepdims=True)

        sums = lax.fori_loop(0, rows_here // tile_rows, body, jnp.zeros((1, 2 * BW), F32))
        esend[pair] = jnp.concatenate(
            [sums[:, 128 * part : 128 * (part + 1)] for part in range(4)]
            + [jnp.zeros((4, 128), F32)],
            0,
        )

    spread(core, rsend)
    rotate(core)
    to_sibling_r.wait_recv()
    spread(1 - core, rrecv)
    rotate(1 - core)

    stores = []
    for pair in range(2):
        store = pltpu.make_async_copy(
            lefts.at[pair], out_hbm.at[:, pl.ds(pair * 2 * BW, BW)], store_sem.at[pair]
        )
        store.start()
        stores.append(store)
    e_sibling = remote(esend, epeer, e_s.at[0], e_r.at[0], sibling)
    e_sibling.start()

    slots = []
    for first, second in zip((2, 3, 0, 1, 4, 5, 6, 7), (4, 5, 6, 7, 2, 3, 0, 1)):
        slot = ps_ref[first + side * (second - first)]
        low_side = jnp.where(slot < 2, slot + 2, jnp.where(slot < 4, slot - 2, slot))
        high_side = jnp.where(slot < 2, slot + 6, jnp.where(slot < 4, slot + 2, slot - 4))
        slots.append(jnp.where(side == 0, low_side, high_side))

    def ranks(order, wanted):
        count = jnp.int32(0)
        result = {}
        for position in order:
            result[position] = count
            count = count + jnp.where(wanted(slots[position]), 1, 0)
        return result

    def source_of(order, wanted, rank, entry, default):
        found = default
        for position in order:
            hit = wanted(slots[position]) & (rank[position] == entry) if rank else wanted(slots[position])
            found = jnp.where(hit, order[position], found)
        return found

    crosses = lambda slot: slot >= 4
    returns = lambda slot: slot < 4
    outward = lambda slot: (slot == 2) | (slot == 3)
    zero = jnp.int32(0)
    send_rank = ranks((0, 1, 2, 3), crosses)
    recv_rank = ranks((4, 5, 6, 7), returns)
    out_rank = ranks((0, 1, 4, 5, 6, 7), outward)
    mid_from = [
        source_of({0: 0, 1: 1, 2: 2, 3: 3}, crosses, send_rank, entry, zero) for entry in range(cap)
    ]
    out_places = {0: 0, 1: 1, 4: 2 + recv_rank[4], 5: 2 + recv_rank[5], 6: 2 + recv_rank[6], 7: 2 + recv_rank[7]}
    out_from = [source_of(out_places, outward, out_rank, entry, zero) for entry in range(2)]
    inner_places = {0: 0, 1: 1, 2: 2, 3: 3, 4: 4 + recv_rank[4], 5: 4 + recv_rank[5], 6: 4 + recv_rank[6], 7: 4 + recv_rank[7]}
    outer_places = {2: 0, 3: 1, 0: 2 + out_rank[0], 1: 2 + out_rank[1], 4: 2 + out_rank[4], 5: 2 + out_rank[5], 6: 2 + out_rank[6], 7: 2 + out_rank[7]}
    inner_from = [
        source_of(inner_places, functools.partial(lax.eq, jnp.int32(entry)), None, entry, zero)
        for entry in range(2)
    ]
    outer_from = [
        source_of(outer_places, functools.partial(lax.eq, jnp.int32(2 + entry)), None, entry, zero)
        for entry in range(2)
    ]

    def piece(index):
        return pl.ds(pl.multiple_of(index * CHUNK, CHUNK), CHUNK)

    def in_copy(index):
        return remote(
            rights.at[:, piece(index)], from_outer.at[:, piece(index)],
            in_s.at[index], in_r.at[index], inner_peer,
        )

    def in_arrival(index):
        return remote(
            rights.at[:, piece(index)], from_outer.at[:, piece(index)],
            in_s.at[index], in_r.at[index], outer_peer,
        )

    def mid_copy(index):
        return remote(
            mid_stage.at[:, piece(index)], from_mid.at[:, piece(index)],
            mid_s.at[index], mid_r.at[index], mid_peer,
        )

    def out_copy(index):
        return remote(
            out_stage.at[:, piece(index)], from_inner.at[:, piece(index)],
            out_s.at[index], out_r.at[index], outer_peer,
        )

    def out_arrival(index):
        return remote(
            out_stage.at[:, piece(index)], from_inner.at[:, piece(index)],
            out_s.at[index], out_r.at[index], inner_peer,
        )

    def inner_forward(index):
        in_arrival(index).wait_recv()
        rows = piece(index)
        options = [rights[0, rows, :], rights[1, rows, :], from_outer[0, rows, :], from_outer[1, rows, :]]
        for entry in range(cap):
            mid_stage[entry, rows, :] = pick(options, mid_from[entry])
        mid_copy(index).start()

    def inner_return(index):
        mid_copy(index).wait_recv()
        rows = piece(index)
        near = [rights[0, rows, :], rights[1, rows, :]]
        beyond = [from_mid[entry, rows, :] for entry in range(cap)]
        for entry in range(2):
            out_stage[entry, rows, :] = pick(near + beyond, out_from[entry])
        out_copy(index).start()
        options = near + [from_outer[0, rows, :], from_outer[1, rows, :]] + beyond
        for entry in range(2):
            fin[entry, rows, :] = pick(options, inner_from[entry])

    def outer_finish(index):
        out_arrival(index).wait_recv()
        rows = piece(index)
        options = [rights[0, rows, :], rights[1, rows, :], from_inner[0, rows, :], from_inner[1, rows, :]]
        for entry in range(2):
            fin[entry, rows, :] = pick(options, outer_from[entry])

    @pl.when(is_outer)
    def _():
        @pl.loop(0, chunks)
        def _(index):
            in_copy(index).start()

    @pl.when(is_inner)
    def _():
        @pl.loop(0, LAG)
        def _(index):
            inner_forward(index)

    def advance(first, last):
        @pl.when(is_inner)
        def _():
            @pl.loop(first, last)
            def _(index):
                @pl.when(index < chunks - LAG)
                def _():
                    inner_forward(index + LAG)

                inner_return(index)

        @pl.when(is_outer)
        def _():
            @pl.loop(first, last)
            def _(index):
                outer_finish(index)

    def exy_copy(step):
        return remote(exy.at[xy], exy.at[xy], exy_s.at[step], exy_r.at[xy], plane_peer(step))

    def exy_arrival(step):
        source = (xy + step) % XY
        return remote(exy.at[source], exy.at[source], exy_s.at[step], exy_r.at[source], plane_peer(step))

    first_cut = chunks // 8
    second_cut = chunks // 2 + chunks // 16
    advance(0, first_cut)
    e_sibling.wait_recv()
    exy[xy] = esend[...] + epeer[...]

    @pl.loop(1, XY)
    def _(step):
        exy_copy(step).start()

    advance(first_cut, second_cut)

    @pl.loop(1, XY)
    def _(step):
        exy_arrival(step).wait_recv()

    plane_sum = exy[0]
    for chip in range(1, XY):
        plane_sum = plane_sum + exy[chip]
    ez[0] = plane_sum
    e_far = remote(ez.at[0], ez.at[1], e_s.at[1], e_r.at[1], far)
    e_far.start()
    advance(second_cut, chunks)
    for pair in range(2):
        store = pltpu.make_async_copy(
            fin.at[pair], out_hbm.at[:, pl.ds(pair * 2 * BW + BW, BW)], store_sem.at[2 + pair]
        )
        store.start()
        stores.append(store)
    e_far.wait_recv()
    energies = (ez[0] + ez[1]) / (4 * XY * rows_here)
    en_ref[0:4, :] = energies[0, 0:4, :]
    en_ref[4:8, :] = energies[1, 0:4, :]

    to_sibling.wait_send()
    to_sibling_r.wait_send()
    to_far.wait_send()
    e_sibling.wait_send()
    e_far.wait_send()

    @pl.loop(1, XY)
    def _(step):
        rs_copy(step).wait_send()
        ag_copy(step).wait_send()
        exy_copy(step).wait_send()

    @pl.when(is_outer)
    def _():
        @pl.loop(0, chunks)
        def _(index):
            in_copy(index).wait_send()

    @pl.when(is_inner)
    def _():
        @pl.loop(0, chunks)
        def _(index):
            mid_copy(index).wait_send()
            out_copy(index).wait_send()

    for store in stores:
        store.wait()


def call(cap, snapshots, partner_slot):
    rows = snapshots.shape[0]
    chunks = rows // CHUNK
    block = (rows, BW)
    dma = pltpu.SemaphoreType.DMA
    scratch = [
        pltpu.VMEM((2, rows, 2 * BW), F32),
        pltpu.VMEM((2, rows, 2 * BW), BF16),
        pltpu.VMEM((2, rows, 2 * BW), BF16),
        pltpu.VMEM((2, 2 * BW, 2 * BW), BF16),
        pltpu.VMEM((2, 2 * BW, 2 * BW), BF16),
        pltpu.VMEM((2, *block), F32),
        pltpu.VMEM((2, *block), F32),
        pltpu.VMEM((2, *block), F32),
        pltpu.VMEM((XY, 40, 128), F32),
        pltpu.VMEM((XY, 40, 128), F32),
        pltpu.VMEM((XY, 40, 128), F32),
        pltpu.VMEM((XY, 40, 128), F32),
        pltpu.VMEM((40, 128), F32),
        pltpu.VMEM((40, 128), F32),
        pltpu.VMEM((XY, 32, 128), F32),
        pltpu.VMEM((3, BW, BW), F32),
        pltpu.VMEM((3, BW, BW), F32),
        pltpu.VMEM((2, 8, 128), F32),
        pltpu.VMEM((2, 8, 128), F32),
        pltpu.VMEM((XY, 2, 8, 128), F32),
        pltpu.VMEM((2, 2, 8, 128), F32),
        pltpu.VMEM((cap, *block), F32),
        pltpu.VMEM((2, *block), F32),
        pltpu.VMEM((2, *block), F32),
        pltpu.VMEM((cap, *block), F32),
        pltpu.VMEM((2, *block), F32),
        dma((2,)), dma((4,)), dma, dma, dma((XY,)), dma((XY,)), dma, dma,
        dma((XY,)), dma((XY,)), dma, dma,
        dma((2,)), dma((2,)), dma((XY,)), dma((XY,)),
        dma((chunks,)), dma((chunks,)), dma((chunks,)), dma((chunks,)), dma((chunks,)), dma((chunks,)),
    ]
    return pl.pallas_call(
        functools.partial(kernel, cap, chunks),
        out_shape=(
            jax.ShapeDtypeStruct(snapshots.shape, F32),
            jax.ShapeDtypeStruct((8, 128), F32),
        ),
        in_specs=[pl.BlockSpec(memory_space=pl.ANY), pl.BlockSpec(memory_space=pltpu.SMEM)],
        out_specs=(pl.BlockSpec(memory_space=pl.ANY), pl.BlockSpec(memory_space=pltpu.VMEM)),
        scratch_shapes=scratch,
        name=f"round_{cap}",
        compiler_params=pltpu.CompilerParams(
            collective_id=cap, has_side_effects=True, vmem_limit_bytes=48 << 20
        ),
    )(snapshots, partner_slot)


def on_device(snapshots, partner_slot):
    crossing = jnp.sum((partner_slot[:4] >= 4).astype(jnp.int32))
    moved, energies = lax.cond(
        crossing <= 2,
        functools.partial(call, 2),
        functools.partial(call, 4),
        snapshots,
        partner_slot,
    )
    return moved, energies.reshape(-1)


def solution(mesh):
    in_specs = (P("rows", "cols"), P())
    out_specs = (P("rows", "cols"), P("cols"))
    return jax.shard_map(
        on_device, mesh=mesh, in_specs=in_specs, out_specs=out_specs, check_vma=False
    )
```

```python
import functools
import types

import jax
import jax.numpy as jnp
from jax import lax
from jax.experimental import pallas as pl
from jax.experimental.pallas import tpu as pltpu
from jax.sharding import PartitionSpec as P

BW = 256
SWEEPS = 4
MESH = pl.DeviceIdType.MESH
F32 = jnp.float32
BF16 = jnp.bfloat16
XY = 16
RAW_CHUNK = 16
LATE_CHUNK = 16
RAW_FIRST = {2: 4, 3: 3, 4: 2}
RAW_ROWS = {2: 192, 3: 128, 4: 96}


def split(value):
    high = value.astype(BF16)
    return high, (value - high.astype(F32)).astype(BF16)


def dot(left, right, contract=((1,), (0,))):
    return lax.dot_general(left, right, (contract, ((), ())), preferred_element_type=F32)


def dot3(left, right, contract=((1,), (0,))):
    return dot(left[0], right[0], contract) + (
        dot(left[0], right[1], contract) + dot(left[1], right[0], contract)
    )


def coupling_of(pieces, diag_tile):
    cross = jnp.concatenate(
        [pieces[:, 0:16, :].reshape(BW, 128), pieces[:, 16:32, :].reshape(BW, 128)], 1
    )
    left_cols = []
    right_rows = []
    for half in range(2):
        left_row = jnp.broadcast_to(diag_tile[half : half + 1, :], (128, 128))
        left_cols.append(jnp.transpose(left_row))
        right_rows.append(diag_tile[2 + half : 3 + half, :])
    left = jnp.concatenate([jnp.concatenate([part, part], 1) for part in left_cols], 0)
    right = jnp.broadcast_to(jnp.concatenate(right_rows, 1), (BW, BW))
    gap = right - left
    coupling = cross * gap / (gap * gap + 4.0 * cross * cross + 0.25 * left * right)
    scale = lax.rsqrt(jnp.full((1, 1), 1.0, F32) + 2.0 * jnp.sum(coupling * coupling))
    return coupling, scale


def polynomials(starts, scale, between):
    eye = (
        lax.broadcasted_iota(jnp.int32, (BW, BW), 0) == lax.broadcasted_iota(jnp.int32, (BW, BW), 1)
    ).astype(F32)
    squares = [(eye + start) * (scale * scale) for start in starts]
    totals = []
    for sweep in range(SWEEPS):
        steps = [1.5 * eye - 0.5 * square for square in squares]
        step_parts = [split(step) for step in steps]
        if sweep == 0:
            totals = [scale * step for step in steps]
            halves = [dot3(split(square), step) for square, step in zip(squares, step_parts)]
        elif sweep == SWEEPS - 1:
            return [dot3(split(total), step) for total, step in zip(totals, step_parts)]
        else:
            stacks = [jnp.concatenate(parts, 0) for parts in zip(totals, squares)]
            stacks = [dot3(split(stack), step) for stack, step in zip(stacks, step_parts)]
            totals = [stack[:BW] for stack in stacks]
            halves = [stack[BW:] for stack in stacks]
        squares = [dot3(split(half), step) for half, step in zip(halves, step_parts)]
        between(sweep)


def pick(options, index):
    value = options[0]
    for position in range(1, len(options)):
        value = jnp.where(index == position, options[position], value)
    return value


def remote(src, dst, send, recv, device):
    return pltpu.make_async_remote_copy(
        src_ref=src, dst_ref=dst, send_sem=send, recv_sem=recv, device_id=device, device_id_type=MESH
    )


def row_of(values):
    return jnp.concatenate(
        [values[:, 128 * part : 128 * (part + 1)] for part in range(4)] + [jnp.zeros((4, 128), F32)], 0
    )


class Stream:
    def __init__(self, whole, near, first, count, chunk, refs, routes, put, fin_first, place):
        self.whole = whole
        self.forwards = self.backs = 0
        self.near, self.first, self.count, self.chunk, self.refs = near, first, count, chunk, refs
        self.routes, self.put, self.fin_first, self.place = routes, put, fin_first, place

    def rows(self, index, offset=0):
        return pl.ds(pl.multiple_of(offset + index * self.chunk, self.chunk), self.chunk)

    def near_rows(self, index):
        return self.rows(index, self.first)

    def in_copy(self, index, device):
        refs = self.refs
        return remote(
            self.near.at[:, self.near_rows(index)], refs.from_outer.at[:, self.rows(index)],
            refs.in_s, refs.in_r.at[index], device,
        )

    def mid_copy(self, index):
        refs = self.refs
        return remote(
            refs.mid_stage.at[:, self.rows(index)], refs.from_mid.at[:, self.rows(index)],
            refs.mid_s, refs.mid_r.at[index], self.place.mid_peer,
        )

    def out_copy(self, index, device):
        refs = self.refs
        return remote(
            refs.out_stage.at[:, self.rows(index)], refs.from_inner.at[:, self.rows(index)],
            refs.out_s, self.out_sem(index), device,
        )

    def out_sem(self, index):
        return self.refs.out_r if self.whole else self.refs.out_r.at[index]

    def near_options(self, index):
        return [self.near[entry, self.near_rows(index), :] for entry in range(2)]

    def forward(self, index):
        self.in_copy(index, self.place.outer_peer).wait_recv()
        rows = self.rows(index)
        refs = self.refs
        options = self.near_options(index) + [refs.from_outer[entry, rows, :] for entry in range(2)]
        for entry in range(refs.mid_stage.shape[0]):
            refs.mid_stage[entry, rows, :] = pick(options, self.routes.mid[entry])
        self.mid_copy(index).start()

    def back(self, index):
        self.mid_copy(index).wait_recv()
        rows = self.rows(index)
        refs = self.refs
        near = self.near_options(index)
        beyond = [refs.from_mid[entry, rows, :] for entry in range(refs.from_mid.shape[0])]
        for entry in range(2):
            refs.out_stage[entry, rows, :] = pick(near + beyond, self.routes.out[entry])
        self.out_copy(index, self.place.outer_peer).start()
        options = near + [refs.from_outer[entry, rows, :] for entry in range(2)] + beyond
        for entry in range(2):
            self.put(entry, self.rows(index, self.fin_first), pick(options, self.routes.inner[entry]))

    def arrive(self, index):
        if not self.whole:
            self.out_copy(index, self.place.inner_peer).wait_recv()
        rows = self.rows(index)
        options = self.near_options(index) + [self.refs.from_inner[entry, rows, :] for entry in range(2)]
        for entry in range(2):
            self.put(entry, self.rows(index, self.fin_first), pick(options, self.routes.outer[entry]))

    def send(self, first, last):
        @pl.when(self.place.is_outer)
        def _():
            @pl.loop(first, last)
            def _(index):
                self.in_copy(index, self.place.inner_peer).start()

    def go(self, forwards, backs):
        forwards = max(self.forwards, min(forwards, self.count))
        backs = max(self.backs, min(backs, forwards))

        @pl.when(self.place.is_inner)
        def _():
            pl.loop(self.forwards, forwards)(self.forward)
            pl.loop(self.backs, backs)(self.back)

        self.forwards, self.backs = forwards, backs

    def finish(self):
        ahead = self.forwards - self.backs
        first, last = self.backs, self.count - ahead

        @pl.when(self.place.is_inner)
        def _():
            @pl.loop(first, last)
            def _(index):
                self.back(index)
                self.forward(index + ahead)

        self.forwards, self.backs = self.count, last
        self.go(self.count, self.count)

    def arrivals(self):
        @pl.when(self.place.is_outer)
        def _():
            if self.whole:
                refs = self.refs
                remote(
                    refs.out_stage, refs.from_inner, refs.out_s, refs.out_r, self.place.inner_peer
                ).wait_recv()
            pl.loop(0, self.count)(self.arrive)

    def drain(self):
        refs, place = self.refs, self.place

        @pl.when(place.is_outer)
        def _():
            sent = self.near.at[:, pl.ds(self.first, self.count * self.chunk)]
            remote(sent, refs.from_outer, refs.in_s, refs.in_r.at[0], place.inner_peer).wait_send()

        @pl.when(place.is_inner)
        def _():
            remote(refs.mid_stage, refs.from_mid, refs.mid_s, refs.mid_r.at[0], place.mid_peer).wait_send()
            remote(
                refs.out_stage, refs.from_inner, refs.out_s, self.out_sem(0), place.outer_peer
            ).wait_send()


def routes_of(ps_ref, side, cap):
    slots = []
    for first, second in zip((2, 3, 0, 1, 4, 5, 6, 7), (4, 5, 6, 7, 2, 3, 0, 1)):
        slot = ps_ref[first + side * (second - first)]
        low_side = jnp.where(slot < 2, slot + 2, jnp.where(slot < 4, slot - 2, slot))
        high_side = jnp.where(slot < 2, slot + 6, jnp.where(slot < 4, slot + 2, slot - 4))
        slots.append(jnp.where(side == 0, low_side, high_side))
    crosses = lambda slot: slot >= 4
    returns = lambda slot: slot < 4
    outward = lambda slot: (slot == 2) | (slot == 3)

    def ranks(order, wanted):
        count = jnp.int32(0)
        result = {}
        for position in order:
            result[position] = count
            count = count + jnp.where(wanted(slots[position]), 1, 0)
        return result

    def source_of(places, wanted):
        found = jnp.int32(0)
        for position, place in places.items():
            found = jnp.where(wanted(position), place, found)
        return found

    send_rank = ranks((0, 1, 2, 3), crosses)
    recv_rank = ranks((4, 5, 6, 7), returns)
    out_rank = ranks((0, 1, 4, 5, 6, 7), outward)
    far_places = {position: recv_rank[position] for position in (4, 5, 6, 7)}
    mid_places = {position: position for position in range(4)}
    out_places = {0: 0, 1: 1, **{position: 2 + place for position, place in far_places.items()}}
    inner_places = {**mid_places, **{position: 4 + place for position, place in far_places.items()}}
    outer_places = {2: 0, 3: 1, **{position: 2 + rank for position, rank in out_rank.items()}}
    return types.SimpleNamespace(
        mid=[
            source_of(mid_places, lambda p: crosses(slots[p]) & (send_rank[p] == entry))
            for entry in range(cap)
        ],
        out=[
            source_of(out_places, lambda p: outward(slots[p]) & (out_rank[p] == entry))
            for entry in range(2)
        ],
        inner=[source_of(inner_places, lambda p: slots[p] == entry) for entry in range(2)],
        outer=[source_of(outer_places, lambda p: slots[p] == 2 + entry) for entry in range(2)],
    )


def kernel(cap, names, x_hbm, ps_ref, out_ref, en_ref, *scratch):
    refs = types.SimpleNamespace(**dict(zip(names, scratch)))
    own, xh, xl, rh, rl = refs.own, refs.xh, refs.xl, refs.rh, refs.rl
    rows_here = own.shape[1]
    raw_rows = refs.raw_fin.shape[1]
    row = lax.axis_index("rows")
    z = lax.axis_index("cols")
    core = row % 2
    xy = (row // 2) % XY
    zh = row // (2 * XY)
    side = z // 2
    place = types.SimpleNamespace(
        is_outer=(z % 3) == 0,
        is_inner=(z % 3) != 0,
        inner_peer={"cols": 1 + z // 3},
        outer_peer={"cols": (3 * z + 1) % 4},
        mid_peer={"cols": 3 - z},
    )
    sibling = {"rows": row + 1 - 2 * core}
    far = {"rows": (row + 2 * XY) % (4 * XY)}

    def plane_peer(step):
        return {"rows": zh * 2 * XY + ((xy + step) % XY) * 2 + core}

    def z_peer(step):
        return {"cols": (z + step) % 4}

    def greet(device):
        pl.semaphore_signal(barrier, inc=1, device_id=device, device_id_type=MESH)

    def load(pair):
        where = pl.ds(pl.multiple_of(pair * 2 * BW, 2 * BW), 2 * BW)
        return pltpu.make_async_copy(x_hbm.at[:, where], own.at[pair], refs.load_sem.at[pair])

    load(1 - core).start()
    load(core).start()
    barrier = pltpu.get_barrier_semaphore()
    greet(sibling)
    greet(far)

    @pl.loop(1, XY)
    def _(step):
        greet(plane_peer(step))

    @pl.loop(1, 4)
    def _(step):
        greet(z_peer(step))

    routes = routes_of(ps_ref, side, cap)
    raw_refs = types.SimpleNamespace(**{n[4:]: r for n, r in vars(refs).items() if n.startswith("raw_")})
    late_refs = types.SimpleNamespace(**{n[5:]: r for n, r in vars(refs).items() if n.startswith("late_")})
    raw_count = raw_rows // RAW_CHUNK
    late_count = (rows_here - raw_rows) // LATE_CHUNK
    def column(pair, half):
        return pl.ds(pl.multiple_of(pair * 2 * BW + half * BW, BW), BW)

    def put_raw(entry, rows, value):
        refs.raw_fin[entry, rows, :] = value

    def put_late(entry, rows, value):
        out_ref[rows, column(entry, 1)] = value

    raw = Stream(True, own, 0, raw_count, RAW_CHUNK, raw_refs, routes, put_raw, 0, place)
    late = Stream(False, refs.rights, 0, late_count, LATE_CHUNK, late_refs, routes, put_late, raw_rows, place)
    first_batch = RAW_FIRST[cap]

    def go_raw(forwards, backs):
        raw.go(first_batch + forwards * 2 // cap, first_batch + backs * 2 // cap)

    def go_late(forwards, backs):
        late.go(forwards * 2 // cap, backs * 2 // cap)

    def gram(pair, target):
        load(pair).wait()
        high, low = split(own[pair])
        xh[pair] = high
        xl[pair] = low
        rows = ((0,), (0,))
        cross = dot3((high[:, :BW], low[:, :BW]), (high[:, BW:], low[:, BW:]), rows)
        target[:, 0:16, :] = cross[:, :128].reshape(XY, 16, 128)
        target[:, 16:32, :] = cross[:, 128:].reshape(XY, 16, 128)
        values = own[pair]
        tile = row_of(jnp.sum(values * values, axis=0, keepdims=True))
        target[:, 32:40, :] = jnp.broadcast_to(tile[None], (XY, 8, 128))

    gmine, gsend, gpeer, rs = refs.gmine, refs.gsend, refs.gpeer, refs.rs
    gram(1 - core, gsend)
    pl.semaphore_wait(barrier, 20)
    to_sibling = remote(gsend, gpeer, refs.pair_s, refs.pair_r, sibling)
    to_sibling.start()

    gram(core, gmine)
    raw.send(0, first_batch)
    to_sibling.wait_recv()
    gmine[...] = gmine[...] + gpeer[...]

    def rs_copy(step):
        target = (xy + step) % XY
        return remote(gmine.at[target], rs.at[xy], refs.rs_s, refs.rs_r, plane_peer(step))

    def gather_copy(buffer, send, recv):
        return lambda step: remote(buffer.at[xy], buffer.at[xy], send, recv, plane_peer(step))

    def start_all(copy, last=XY):
        @pl.loop(1, last)
        def _(step):
            copy(step).start()

    def others(buffer, send, recv, device, last=XY):
        part = buffer.at[pl.ds(0, last - 1)]
        return remote(part, part, send, recv, device)

    start_all(rs_copy)
    rs[xy] = gmine[xy]

    raw.go(first_batch, 0)
    others(rs, refs.rs_s, refs.rs_r, plane_peer(1)).wait_recv()
    total = rs[0]
    for chip in range(1, XY):
        total = total + rs[chip]
    refs.zsend[...] = total
    to_far = remote(refs.zsend, refs.zrecv, refs.z_s, refs.z_r, far)
    to_far.start()
    to_far.wait_recv()
    total = refs.zsend[...] + refs.zrecv[...]
    diag_tile = total[32:40, :]
    ag, zl, fp, fag = refs.ag, refs.zl, refs.fp, refs.fag
    ag[xy] = total[0:32, :]
    zl[z] = total
    ag_copy = gather_copy(ag, refs.ag_s, refs.ag_r)
    start_all(ag_copy)

    def zl_copy(step):
        return remote(zl.at[z], zl.at[z], refs.zl_s, refs.zl_r, z_peer(step))

    start_all(zl_copy, 4)
    raw.send(first_batch, raw_count)
    go_raw(0, 0)
    go_raw(1, 0)
    others(ag, refs.ag_s, refs.ag_r, plane_peer(1)).wait_recv()

    coupling, scale = coupling_of(ag[...], diag_tile)
    coupling_parts = split(coupling)
    outer_product = dot3(coupling_parts, coupling_parts, ((1,), (1,)))
    inner_product = dot3(coupling_parts, coupling_parts, ((0,), (0,)))
    others(zl, refs.zl_s, refs.zl_r, z_peer(1), 4).wait_recv()
    fp[core] = zl[...]
    to_sibling_z = remote(zl, fp.at[core], refs.fp_s, refs.fp_r, sibling)
    to_sibling_z.start()
    fag_copy = gather_copy(fag, refs.fag_s, refs.fag_r)
    incoming_diag = []

    def gather_incoming():
        remote(zl, fp.at[1 - core], refs.fp_s, refs.fp_r, sibling).wait_recv()
        parity, plane = jnp.int32(0), jnp.int32(0)
        for pair in range(8):
            hit = ps_ref[pair] == 2 * z + core
            parity = jnp.where(hit, pair % 2, parity)
            plane = jnp.where(hit, pair // 2, plane)
        incoming = fp[parity, plane]
        fag[xy] = incoming[0:32, :]
        incoming_diag.append(incoming[32:40, :])
        start_all(fag_copy)

    def beside(sweep):
        go_raw(*((3, 0), (4, 1), (5, 2))[sweep])
        if sweep == 1:
            gather_incoming()

    go_raw(2, 0)
    left_part, right_part = polynomials(
        [outer_product, inner_product], scale, beside
    )
    rsend, rrecv = refs.rsend, refs.rrecv
    rsend[1] = right_part
    rsend[0] = dot3(split(left_part), coupling_parts)
    to_sibling_r = remote(
        rsend.at[pl.ds(0, 2)], rrecv.at[pl.ds(0, 2)], refs.ro_s.at[0], refs.ro_r.at[0], sibling
    )
    to_sibling_r.start()
    rsend[2] = left_part
    to_sibling_l = remote(rsend.at[2], rrecv.at[2], refs.ro_s.at[1], refs.ro_r.at[1], sibling)
    to_sibling_l.start()

    def spread(half, pair, blocks):
        for row_block, block in enumerate(blocks):
            high, low = split(block)
            where = (half, pair, pl.ds(row_block * BW, BW))
            rh[where] = high
            rl[where] = low

    rights = refs.rights
    esend, epeer, exy, ez = refs.esend, refs.epeer, refs.exy, refs.ez

    def rotate(half, pair, first, last):
        rows = pl.ds(first, last - first)
        result = dot3((xh[pair, rows, :], xl[pair, rows, :]), (rh[half, pair], rl[half, pair]))
        if half == 0:
            out_ref[rows, column(pair, 0)] = result
        elif first > 0:
            rights[pair] = result
        return jnp.sum(result * result, axis=0, keepdims=True)

    spread(1, core, (rsend[0], rsend[1]))
    right_sums = [rotate(1, core, raw_rows, rows_here)]
    go_raw(6, 3)
    to_sibling_r.wait_recv()
    spread(1, 1 - core, (rrecv[0], rrecv[1]))
    right_sums.append(rotate(1, 1 - core, raw_rows, rows_here))

    late.send(0, late_count)
    go_raw(raw_count, 4)
    to_sibling_l.wait_recv()
    left_sums = []

    def rotate_left(pair, source):
        spread(0, pair, (source[2], -jnp.transpose(source[0])))
        left_sums.append(rotate(0, pair, 0, rows_here))

    rotate_left(core, rsend)
    rotate_left(1 - core, rrecv)
    go_raw(raw_count, 5)
    for entry, pair in enumerate((core, 1 - core)):
        sums = right_sums[entry] + rotate(1, pair, 0, raw_rows)
        esend[pair] = row_of(jnp.concatenate([left_sums[entry], sums], 1))
    e_sibling = remote(esend, epeer, refs.e_s.at[0], refs.e_r.at[0], sibling)
    e_sibling.start()
    go_raw(raw_count, 6)
    go_late(2, 0)
    raw.go(raw_count, raw_count)

    others(fag, refs.fag_s, refs.fag_r, plane_peer(1)).wait_recv()
    fsend, frecv, fh, fl = refs.fsend, refs.frecv, refs.fh, refs.fl
    coupling, scale = coupling_of(fag[...], incoming_diag[0])
    coupling_parts = split(coupling)
    e_sibling.wait_recv()
    exy[xy] = esend[...] + epeer[...]
    exy_copy = gather_copy(exy, refs.exy_s, refs.exy_r)
    start_all(exy_copy)
    go_late(7, 0)
    inner_product = dot3(coupling_parts, coupling_parts, ((0,), (0,)))
    go_late(8, 1)
    (right_part,) = polynomials(
        [inner_product], scale, lambda sweep: go_late(*((9, 3), (11, 5), (12, 6))[sweep])
    )
    fsend[1] = right_part
    fsend[0] = dot3(coupling_parts, split(right_part))
    to_sibling_f = remote(fsend, frecv, refs.f_s, refs.f_r, sibling)
    to_sibling_f.start()
    raw.arrivals()
    go_late(14, 8)
    others(exy, refs.exy_s, refs.exy_r, plane_peer(1)).wait_recv()
    plane_sum = exy[0]
    for chip in range(1, XY):
        plane_sum = plane_sum + exy[chip]
    ez[0] = plane_sum
    e_far = remote(ez.at[0], ez.at[1], refs.e_s.at[1], refs.e_r.at[1], far)
    e_far.start()

    def finish_raw(slot, source):
        for block in range(2):
            high, low = split(source[block])
            fh[slot, pl.ds(block * BW, BW), :] = high
            fl[slot, pl.ds(block * BW, BW), :] = low
        out_ref[pl.ds(0, raw_rows), column(slot, 1)] = dot3(split(refs.raw_fin[slot]), (fh[slot], fl[slot]))

    finish_raw(core, fsend)
    go_late(17, 11)
    to_sibling_f.wait_recv()
    finish_raw(1 - core, frecv)
    late.finish()
    late.arrivals()
    e_far.wait_recv()
    energies = (ez[0] + ez[1]) / (4 * XY * rows_here)
    en_ref[0:4, :] = energies[0, 0:4, :]
    en_ref[4:8, :] = energies[1, 0:4, :]

    for copy in (to_sibling, to_sibling_r, to_sibling_l, to_sibling_z, to_sibling_f, to_far, e_sibling, e_far):
        copy.wait_send()

    for buffer, send, recv in (
        (rs, refs.rs_s, refs.rs_r), (ag, refs.ag_s, refs.ag_r), (fag, refs.fag_s, refs.fag_r), (exy, refs.exy_s, refs.exy_r)
    ):
        others(buffer, send, recv, plane_peer(1)).wait_send()
    others(zl, refs.zl_s, refs.zl_r, z_peer(1), 4).wait_send()
    raw.drain()
    late.drain()


def call(cap, snapshots, partner_slot):
    rows = snapshots.shape[0]
    raw_rows = RAW_ROWS[cap]
    dma = pltpu.SemaphoreType.DMA
    f32 = lambda *shape: pltpu.VMEM(shape, F32)
    b16 = lambda *shape: pltpu.VMEM(shape, BF16)
    scratch = dict(
        own=f32(2, rows, 2 * BW), xh=b16(2, rows, 2 * BW), xl=b16(2, rows, 2 * BW),
        rh=b16(2, 2, 2 * BW, BW), rl=b16(2, 2, 2 * BW, BW),
        rights=f32(2, rows - raw_rows, BW),
        gmine=f32(XY, 40, 128), gsend=f32(XY, 40, 128), gpeer=f32(XY, 40, 128), rs=f32(XY, 40, 128),
        zsend=f32(40, 128), zrecv=f32(40, 128), ag=f32(XY, 32, 128),
        zl=f32(4, 40, 128), fp=f32(2, 4, 40, 128), fag=f32(XY, 32, 128),
        rsend=f32(3, BW, BW), rrecv=f32(3, BW, BW),
        fsend=f32(2, BW, BW), frecv=f32(2, BW, BW), fh=b16(2, 2 * BW, BW), fl=b16(2, 2 * BW, BW),
        esend=f32(2, 8, 128), epeer=f32(2, 8, 128), exy=f32(XY, 2, 8, 128), ez=f32(2, 2, 8, 128),
        load_sem=dma((2,)), pair_s=dma, pair_r=dma, rs_s=dma, rs_r=dma,
        z_s=dma, z_r=dma, ag_s=dma, ag_r=dma, zl_s=dma, zl_r=dma,
        fp_s=dma, fp_r=dma, fag_s=dma, fag_r=dma, ro_s=dma((2,)), ro_r=dma((2,)), f_s=dma, f_r=dma,
        e_s=dma((2,)), e_r=dma((2,)), exy_s=dma, exy_r=dma,
        raw_fin=f32(2, raw_rows, 2 * BW),
    )
    for name, height, width, chunk in (
        ("raw", raw_rows, 2 * BW, RAW_CHUNK), ("late", rows - raw_rows, BW, LATE_CHUNK)
    ):
        for buffer, blocks in (("mid_stage", cap), ("from_mid", cap), ("out_stage", 2), ("from_outer", 2), ("from_inner", 2)):
            scratch[f"{name}_{buffer}"] = f32(blocks, height, width)
        for sem in ("in_s", "mid_s", "out_s"):
            scratch[f"{name}_{sem}"] = dma
        for sem in ("in_r", "mid_r", "out_r"):
            scratch[f"{name}_{sem}"] = dma((height // chunk,))
    scratch["raw_out_r"] = dma
    return pl.pallas_call(
        functools.partial(kernel, cap, tuple(scratch)),
        out_shape=(
            jax.ShapeDtypeStruct(snapshots.shape, F32),
            jax.ShapeDtypeStruct((8, 128), F32),
        ),
        in_specs=[pl.BlockSpec(memory_space=pl.ANY), pl.BlockSpec(memory_space=pltpu.SMEM)],
        out_specs=(pl.BlockSpec(memory_space=pltpu.VMEM), pl.BlockSpec(memory_space=pltpu.VMEM)),
        scratch_shapes=list(scratch.values()),
        name=f"round_{cap}",
        compiler_params=pltpu.CompilerParams(
            collective_id=cap, has_side_effects=True, vmem_limit_bytes=48 << 20
        ),
    )(snapshots, partner_slot)


def on_device(snapshots, partner_slot):
    crossing = jnp.sum((partner_slot[:4] >= 4).astype(jnp.int32))
    moved, energies = lax.switch(
        jnp.maximum(crossing, 2) - 2,
        [functools.partial(call, cap) for cap in (2, 3, 4)],
        snapshots,
        partner_slot,
    )
    return moved, energies.reshape(-1)


def solution(mesh):
    in_specs = (P("rows", "cols"), P())
    out_specs = (P("rows", "cols"), P("cols"))
    return jax.shard_map(
        on_device, mesh=mesh, in_specs=in_specs, out_specs=out_specs, check_vma=False
    )
```

```python
import functools
import types

import jax
import jax.numpy as jnp
from jax import lax
from jax.experimental import pallas as pl
from jax.experimental.pallas import tpu as pltpu
from jax.sharding import PartitionSpec as P

BW = 256
SWEEPS = 4
MESH = pl.DeviceIdType.MESH
F32 = jnp.float32
BF16 = jnp.bfloat16
XY = 16
RAW_CHUNK = 16
LATE_CHUNK = 16
RAW_FIRST = {2: 4, 3: 3, 4: 2}
RAW_SENT = {2: 7, 3: 4, 4: 3}
RAW_ROWS = {2: 224, 3: 128, 4: 96}


def split(value):
    high = value.astype(BF16)
    return high, (value - high.astype(F32)).astype(BF16)


def dot(left, right, contract=((1,), (0,))):
    return lax.dot_general(left, right, (contract, ((), ())), preferred_element_type=F32)


def dot3(left, right, contract=((1,), (0,))):
    return dot(left[0], right[0], contract) + (
        dot(left[0], right[1], contract) + dot(left[1], right[0], contract)
    )


def coupling_of(pieces, diag_tile):
    cross = jnp.concatenate(
        [pieces[:, 0:16, :].reshape(BW, 128), pieces[:, 16:32, :].reshape(BW, 128)], 1
    )
    left_cols = []
    right_rows = []
    for half in range(2):
        left_row = jnp.broadcast_to(diag_tile[half : half + 1, :], (128, 128))
        left_cols.append(jnp.transpose(left_row))
        right_rows.append(diag_tile[2 + half : 3 + half, :])
    left = jnp.concatenate([jnp.concatenate([part, part], 1) for part in left_cols], 0)
    right = jnp.broadcast_to(jnp.concatenate(right_rows, 1), (BW, BW))
    gap = right - left
    coupling = cross * gap / (gap * gap + 4.0 * cross * cross + 0.25 * left * right)
    scale = lax.rsqrt(jnp.full((1, 1), 1.0, F32) + 2.0 * jnp.sum(coupling * coupling))
    return coupling, scale


def polynomials(starts, scale, between):
    eye = (
        lax.broadcasted_iota(jnp.int32, (BW, BW), 0) == lax.broadcasted_iota(jnp.int32, (BW, BW), 1)
    ).astype(F32)
    squares = [(eye + start) * (scale * scale) for start in starts]
    totals = []
    for sweep in range(SWEEPS):
        steps = [1.5 * eye - 0.5 * square for square in squares]
        step_parts = [split(step) for step in steps]
        if sweep == 0:
            totals = [scale * step for step in steps]
            halves = [dot3(split(square), step) for square, step in zip(squares, step_parts)]
        elif sweep == SWEEPS - 1:
            return [dot3(split(total), step) for total, step in zip(totals, step_parts)]
        else:
            stacks = [jnp.concatenate(parts, 0) for parts in zip(totals, squares)]
            stacks = [dot3(split(stack), step) for stack, step in zip(stacks, step_parts)]
            totals = [stack[:BW] for stack in stacks]
            halves = [stack[BW:] for stack in stacks]
        squares = [dot3(split(half), step) for half, step in zip(halves, step_parts)]
        between(sweep)


def pick(options, index):
    value = options[0]
    for position in range(1, len(options)):
        value = jnp.where(index == position, options[position], value)
    return value


def remote(src, dst, send, recv, device):
    return pltpu.make_async_remote_copy(
        src_ref=src, dst_ref=dst, send_sem=send, recv_sem=recv, device_id=device, device_id_type=MESH
    )


def row_of(values):
    return jnp.concatenate(
        [values[:, 128 * part : 128 * (part + 1)] for part in range(4)] + [jnp.zeros((4, 128), F32)], 0
    )


class Stream:
    def __init__(self, whole, near, first, count, chunk, refs, routes, put, fin_first, place):
        self.whole = whole
        self.forwards = self.backs = 0
        self.near, self.first, self.count, self.chunk, self.refs = near, first, count, chunk, refs
        self.routes, self.put, self.fin_first, self.place = routes, put, fin_first, place

    def rows(self, index, offset=0):
        return pl.ds(pl.multiple_of(offset + index * self.chunk, self.chunk), self.chunk)

    def near_rows(self, index):
        return self.rows(index, self.first)

    def in_copy(self, index, device):
        refs = self.refs
        return remote(
            self.near.at[:, self.near_rows(index)], refs.from_outer.at[:, self.rows(index)],
            refs.in_s, refs.in_r.at[index], device,
        )

    def mid_copy(self, index):
        refs = self.refs
        return remote(
            refs.mid_stage.at[:, self.rows(index)], refs.from_mid.at[:, self.rows(index)],
            refs.mid_s, refs.mid_r.at[index], self.place.mid_peer,
        )

    def out_copy(self, index, device):
        refs = self.refs
        return remote(
            refs.out_stage.at[:, self.rows(index)], refs.from_inner.at[:, self.rows(index)],
            refs.out_s, self.out_sem(index), device,
        )

    def out_sem(self, index):
        return self.refs.out_r if self.whole else self.refs.out_r.at[index]

    def near_options(self, index):
        return [self.near[entry, self.near_rows(index), :] for entry in range(2)]

    def forward(self, index):
        self.in_copy(index, self.place.outer_peer).wait_recv()
        rows = self.rows(index)
        refs = self.refs
        options = self.near_options(index) + [refs.from_outer[entry, rows, :] for entry in range(2)]
        for entry in range(refs.mid_stage.shape[0]):
            refs.mid_stage[entry, rows, :] = pick(options, self.routes.mid[entry])
        self.mid_copy(index).start()

    def back(self, index):
        self.mid_copy(index).wait_recv()
        rows = self.rows(index)
        refs = self.refs
        near = self.near_options(index)
        beyond = [refs.from_mid[entry, rows, :] for entry in range(refs.from_mid.shape[0])]
        for entry in range(2):
            refs.out_stage[entry, rows, :] = pick(near + beyond, self.routes.out[entry])
        self.out_copy(index, self.place.outer_peer).start()
        options = near + [refs.from_outer[entry, rows, :] for entry in range(2)] + beyond
        for entry in range(2):
            self.put(entry, self.rows(index, self.fin_first), pick(options, self.routes.inner[entry]))

    def arrive(self, index):
        if not self.whole:
            self.out_copy(index, self.place.inner_peer).wait_recv()
        rows = self.rows(index)
        options = self.near_options(index) + [self.refs.from_inner[entry, rows, :] for entry in range(2)]
        for entry in range(2):
            self.put(entry, self.rows(index, self.fin_first), pick(options, self.routes.outer[entry]))

    def send(self, first, last):
        @pl.when(self.place.is_outer)
        def _():
            @pl.loop(first, last)
            def _(index):
                self.in_copy(index, self.place.inner_peer).start()

    def go(self, forwards, backs):
        forwards = max(self.forwards, min(forwards, self.count))
        backs = max(self.backs, min(backs, forwards))

        @pl.when(self.place.is_inner)
        def _():
            pl.loop(self.forwards, forwards)(self.forward)
            pl.loop(self.backs, backs)(self.back)

        self.forwards, self.backs = forwards, backs

    def finish(self):
        ahead = self.forwards - self.backs
        first, last = self.backs, self.count - ahead

        @pl.when(self.place.is_inner)
        def _():
            @pl.loop(first, last)
            def _(index):
                self.back(index)
                self.forward(index + ahead)

        self.forwards, self.backs = self.count, last
        self.go(self.count, self.count)

    def arrivals(self):
        @pl.when(self.place.is_outer)
        def _():
            if self.whole:
                refs = self.refs
                remote(
                    refs.out_stage, refs.from_inner, refs.out_s, refs.out_r, self.place.inner_peer
                ).wait_recv()
            pl.loop(0, self.count)(self.arrive)

    def drain(self):
        refs, place = self.refs, self.place

        @pl.when(place.is_outer)
        def _():
            sent = self.near.at[:, pl.ds(self.first, self.count * self.chunk)]
            remote(sent, refs.from_outer, refs.in_s, refs.in_r.at[0], place.inner_peer).wait_send()

        @pl.when(place.is_inner)
        def _():
            remote(refs.mid_stage, refs.from_mid, refs.mid_s, refs.mid_r.at[0], place.mid_peer).wait_send()
            remote(
                refs.out_stage, refs.from_inner, refs.out_s, self.out_sem(0), place.outer_peer
            ).wait_send()


def routes_of(ps_ref, side, cap):
    slots = []
    for first, second in zip((2, 3, 0, 1, 4, 5, 6, 7), (4, 5, 6, 7, 2, 3, 0, 1)):
        slot = ps_ref[first + side * (second - first)]
        low_side = jnp.where(slot < 2, slot + 2, jnp.where(slot < 4, slot - 2, slot))
        high_side = jnp.where(slot < 2, slot + 6, jnp.where(slot < 4, slot + 2, slot - 4))
        slots.append(jnp.where(side == 0, low_side, high_side))
    crosses = lambda slot: slot >= 4
    returns = lambda slot: slot < 4
    outward = lambda slot: (slot == 2) | (slot == 3)

    def ranks(order, wanted):
        count = jnp.int32(0)
        result = {}
        for position in order:
            result[position] = count
            count = count + jnp.where(wanted(slots[position]), 1, 0)
        return result

    def source_of(places, wanted):
        found = jnp.int32(0)
        for position, place in places.items():
            found = jnp.where(wanted(position), place, found)
        return found

    send_rank = ranks((0, 1, 2, 3), crosses)
    recv_rank = ranks((4, 5, 6, 7), returns)
    out_rank = ranks((0, 1, 4, 5, 6, 7), outward)
    far_places = {position: recv_rank[position] for position in (4, 5, 6, 7)}
    mid_places = {position: position for position in range(4)}
    out_places = {0: 0, 1: 1, **{position: 2 + place for position, place in far_places.items()}}
    inner_places = {**mid_places, **{position: 4 + place for position, place in far_places.items()}}
    outer_places = {2: 0, 3: 1, **{position: 2 + rank for position, rank in out_rank.items()}}
    return types.SimpleNamespace(
        mid=[
            source_of(mid_places, lambda p: crosses(slots[p]) & (send_rank[p] == entry))
            for entry in range(cap)
        ],
        out=[
            source_of(out_places, lambda p: outward(slots[p]) & (out_rank[p] == entry))
            for entry in range(2)
        ],
        inner=[source_of(inner_places, lambda p: slots[p] == entry) for entry in range(2)],
        outer=[source_of(outer_places, lambda p: slots[p] == 2 + entry) for entry in range(2)],
    )


def kernel(cap, names, x_hbm, ps_any, out_ref, en_ref, *scratch):
    refs = types.SimpleNamespace(**dict(zip(names, scratch)))
    own, xh, xl, rh, rl = refs.own, refs.xh, refs.xl, refs.rh, refs.rl
    rows_here = own.shape[1]
    raw_rows = refs.raw_fin.shape[1]
    row = lax.axis_index("rows")
    z = lax.axis_index("cols")
    core = row % 2
    xy = (row // 2) % XY
    zh = row // (2 * XY)
    side = z // 2
    place = types.SimpleNamespace(
        is_outer=(z % 3) == 0,
        is_inner=(z % 3) != 0,
        inner_peer={"cols": 1 + z // 3},
        outer_peer={"cols": (3 * z + 1) % 4},
        mid_peer={"cols": 3 - z},
    )
    sibling = {"rows": row + 1 - 2 * core}
    far = {"rows": (row + 2 * XY) % (4 * XY)}

    def plane_peer(step):
        return {"rows": zh * 2 * XY + ((xy + step) % XY) * 2 + core}

    def z_peer(step):
        return {"cols": (z + step) % 4}

    def greet(device):
        pl.semaphore_signal(barrier, inc=1, device_id=device, device_id_type=MESH)

    def load(pair):
        where = pl.ds(pl.multiple_of(pair * 2 * BW, 2 * BW), 2 * BW)
        return pltpu.make_async_copy(x_hbm.at[:, where], own.at[pair], refs.load_sem.at[pair])

    load(1 - core).start()
    load(core).start()
    ps_ref = refs.slots
    ps_load = pltpu.make_async_copy(ps_any, ps_ref, refs.ps_sem)
    ps_load.start()
    barrier = pltpu.get_barrier_semaphore()
    greet(sibling)
    greet(far)

    @pl.loop(1, XY)
    def _(step):
        greet(plane_peer(step))

    @pl.loop(1, 4)
    def _(step):
        greet(z_peer(step))

    routes = types.SimpleNamespace()
    raw_refs = types.SimpleNamespace(**{n[4:]: r for n, r in vars(refs).items() if n.startswith("raw_")})
    late_refs = types.SimpleNamespace(**{n[5:]: r for n, r in vars(refs).items() if n.startswith("late_")})
    raw_count = raw_rows // RAW_CHUNK
    late_count = (rows_here - raw_rows) // LATE_CHUNK
    def column(pair, half):
        return pl.ds(pl.multiple_of(pair * 2 * BW + half * BW, BW), BW)

    def put_raw(entry, rows, value):
        refs.raw_fin[entry, rows, :] = value

    def put_late(entry, rows, value):
        out_ref[rows, column(entry, 1)] = value

    raw = Stream(True, own, 0, raw_count, RAW_CHUNK, raw_refs, routes, put_raw, 0, place)
    late = Stream(False, refs.rights, 0, late_count, LATE_CHUNK, late_refs, routes, put_late, raw_rows, place)
    first_batch = RAW_FIRST[cap]
    first_sent = RAW_SENT[cap]

    def go_raw(forwards, backs):
        raw.go(first_batch + forwards * 2 // cap, first_batch + backs * 2 // cap)

    def go_late(forwards, backs):
        late.go(forwards * 2 // cap, backs * 2 // cap)

    def gram(pair, target):
        load(pair).wait()
        high, low = split(own[pair])
        xh[pair] = high
        xl[pair] = low
        rows = ((0,), (0,))
        cross = dot3((high[:, :BW], low[:, :BW]), (high[:, BW:], low[:, BW:]), rows)
        target[:, 0:16, :] = cross[:, :128].reshape(XY, 16, 128)
        target[:, 16:32, :] = cross[:, 128:].reshape(XY, 16, 128)
        values = own[pair]
        tile = row_of(jnp.sum(values * values, axis=0, keepdims=True))
        target[:, 32:40, :] = jnp.broadcast_to(tile[None], (XY, 8, 128))

    gmine, gsend, gpeer, rs = refs.gmine, refs.gsend, refs.gpeer, refs.rs
    gram(1 - core, gsend)
    pl.semaphore_wait(barrier, 20)
    to_sibling = remote(gsend, gpeer, refs.pair_s, refs.pair_r, sibling)
    to_sibling.start()

    gram(core, gmine)
    raw.send(0, first_sent)
    to_sibling.wait_recv()
    gmine[...] = gmine[...] + gpeer[...]

    def rs_copy(step):
        target = (xy + step) % XY
        return remote(gmine.at[target], rs.at[xy], refs.rs_s, refs.rs_r, plane_peer(step))

    def gather_copy(buffer, send, recv):
        return lambda step: remote(buffer.at[xy], buffer.at[xy], send, recv, plane_peer(step))

    def start_all(copy, last=XY):
        @pl.loop(1, last)
        def _(step):
            copy(step).start()

    def others(buffer, send, recv, device, last=XY):
        part = buffer.at[pl.ds(0, last - 1)]
        return remote(part, part, send, recv, device)

    start_all(rs_copy)
    rs[xy] = gmine[xy]

    ps_load.wait()
    vars(routes).update(vars(routes_of(ps_ref, side, cap)))
    raw.go(first_batch, 0)
    others(rs, refs.rs_s, refs.rs_r, plane_peer(1)).wait_recv()
    total = rs[0]
    for chip in range(1, XY):
        total = total + rs[chip]
    refs.zsend[...] = total
    to_far = remote(refs.zsend, refs.zrecv, refs.z_s, refs.z_r, far)
    to_far.start()
    to_far.wait_recv()
    total = refs.zsend[...] + refs.zrecv[...]
    diag_tile = total[32:40, :]
    ag, zl, fp, fag = refs.ag, refs.zl, refs.fp, refs.fag
    ag[xy] = total[0:32, :]
    zl[z] = total
    ag_copy = gather_copy(ag, refs.ag_s, refs.ag_r)
    start_all(ag_copy)

    def zl_copy(step):
        return remote(zl.at[z], zl.at[z], refs.zl_s, refs.zl_r, z_peer(step))

    start_all(zl_copy, 4)
    raw.send(first_sent, raw_count)
    go_raw(2, 0)
    go_raw(3, 1)
    others(ag, refs.ag_s, refs.ag_r, plane_peer(1)).wait_recv()

    coupling, scale = coupling_of(ag[...], diag_tile)
    go_raw(4, 2)
    coupling_parts = split(coupling)
    outer_product = dot3(coupling_parts, coupling_parts, ((1,), (1,)))
    inner_product = dot3(coupling_parts, coupling_parts, ((0,), (0,)))
    others(zl, refs.zl_s, refs.zl_r, z_peer(1), 4).wait_recv()
    fp[core] = zl[...]
    to_sibling_z = remote(zl, fp.at[core], refs.fp_s, refs.fp_r, sibling)
    to_sibling_z.start()
    fag_copy = gather_copy(fag, refs.fag_s, refs.fag_r)
    incoming_diag = []

    def gather_incoming():
        remote(zl, fp.at[1 - core], refs.fp_s, refs.fp_r, sibling).wait_recv()
        parity, plane = jnp.int32(0), jnp.int32(0)
        for pair in range(8):
            hit = ps_ref[pair] == 2 * z + core
            parity = jnp.where(hit, pair % 2, parity)
            plane = jnp.where(hit, pair // 2, plane)
        incoming = fp[parity, plane]
        fag[xy] = incoming[0:32, :]
        incoming_diag.append(incoming[32:40, :])
        start_all(fag_copy)

    def beside(sweep):
        go_raw(*((5, 3), (6, 3), (7, 4))[sweep])

    go_raw(5, 2)
    left_part, right_part = polynomials(
        [outer_product, inner_product], scale, beside
    )
    rsend, rrecv = refs.rsend, refs.rrecv
    rsend[1] = right_part
    rsend[0] = dot3(split(left_part), coupling_parts)
    to_sibling_r = remote(
        rsend.at[pl.ds(0, 2)], rrecv.at[pl.ds(0, 2)], refs.ro_s.at[0], refs.ro_r.at[0], sibling
    )
    to_sibling_r.start()
    rsend[2] = left_part
    to_sibling_l = remote(rsend.at[2], rrecv.at[2], refs.ro_s.at[1], refs.ro_r.at[1], sibling)
    to_sibling_l.start()

    def spread(half, pair, blocks):
        for row_block, block in enumerate(blocks):
            high, low = split(block)
            where = (half, pair, pl.ds(row_block * BW, BW))
            rh[where] = high
            rl[where] = low

    rights = refs.rights
    esend, epeer, exy, ez = refs.esend, refs.epeer, refs.exy, refs.ez

    def rotate(half, pair, first, last):
        rows = pl.ds(first, last - first)
        result = dot3((xh[pair, rows, :], xl[pair, rows, :]), (rh[half, pair], rl[half, pair]))
        if half == 0:
            out_ref[rows, column(pair, 0)] = result
        elif first > 0:
            rights[pair] = result
        return jnp.sum(result * result, axis=0, keepdims=True)

    spread(1, core, (rsend[0], rsend[1]))
    right_sums = [rotate(1, core, raw_rows, rows_here)]
    go_raw(9, 5)
    gather_incoming()
    go_raw(10, 6)
    to_sibling_r.wait_recv()
    spread(1, 1 - core, (rrecv[0], rrecv[1]))
    right_sums.append(rotate(1, 1 - core, raw_rows, rows_here))

    late.send(0, late_count)
    go_raw(raw_count, 7)
    to_sibling_l.wait_recv()
    left_sums = []

    def rotate_left(pair, source):
        spread(0, pair, (source[2], -jnp.transpose(source[0])))
        left_sums.append(rotate(0, pair, 0, rows_here))

    rotate_left(core, rsend)
    go_raw(raw_count, 8)
    rotate_left(1 - core, rrecv)
    go_raw(raw_count, 9)
    for entry, pair in enumerate((core, 1 - core)):
        sums = right_sums[entry] + rotate(1, pair, 0, raw_rows)
        esend[pair] = row_of(jnp.concatenate([left_sums[entry], sums], 1))
    e_sibling = remote(esend, epeer, refs.e_s.at[0], refs.e_r.at[0], sibling)
    e_sibling.start()
    go_raw(raw_count, 9)
    go_late(2, 0)
    raw.go(raw_count, raw_count)

    others(fag, refs.fag_s, refs.fag_r, plane_peer(1)).wait_recv()
    fsend, frecv, fh, fl = refs.fsend, refs.frecv, refs.fh, refs.fl
    coupling, scale = coupling_of(fag[...], incoming_diag[0])
    coupling_parts = split(coupling)
    e_sibling.wait_recv()
    exy[xy] = esend[...] + epeer[...]
    exy_copy = gather_copy(exy, refs.exy_s, refs.exy_r)
    start_all(exy_copy)
    go_late(7, 0)
    inner_product = dot3(coupling_parts, coupling_parts, ((0,), (0,)))
    go_late(8, 1)
    (right_part,) = polynomials(
        [inner_product], scale, lambda sweep: go_late(*((9, 3), (11, 5), (12, 6))[sweep])
    )
    fsend[1] = right_part
    fsend[0] = dot3(coupling_parts, split(right_part))
    to_sibling_f = remote(fsend, frecv, refs.f_s, refs.f_r, sibling)
    to_sibling_f.start()
    raw.arrivals()
    go_late(14, 8)
    others(exy, refs.exy_s, refs.exy_r, plane_peer(1)).wait_recv()
    plane_sum = exy[0]
    for chip in range(1, XY):
        plane_sum = plane_sum + exy[chip]
    ez[0] = plane_sum
    e_far = remote(ez.at[0], ez.at[1], refs.e_s.at[1], refs.e_r.at[1], far)
    e_far.start()

    def finish_raw(slot, source):
        for block in range(2):
            high, low = split(source[block])
            fh[slot, pl.ds(block * BW, BW), :] = high
            fl[slot, pl.ds(block * BW, BW), :] = low
        out_ref[pl.ds(0, raw_rows), column(slot, 1)] = dot3(split(refs.raw_fin[slot]), (fh[slot], fl[slot]))

    finish_raw(core, fsend)
    go_late(17, 11)
    to_sibling_f.wait_recv()
    finish_raw(1 - core, frecv)
    late.finish()
    late.arrivals()
    e_far.wait_recv()
    energies = (ez[0] + ez[1]) / (4 * XY * rows_here)
    en_ref[0:4, :] = energies[0, 0:4, :]
    en_ref[4:8, :] = energies[1, 0:4, :]

    for copy in (to_sibling, to_sibling_r, to_sibling_l, to_sibling_z, to_sibling_f, to_far, e_sibling, e_far):
        copy.wait_send()

    for buffer, send, recv in (
        (rs, refs.rs_s, refs.rs_r), (ag, refs.ag_s, refs.ag_r), (fag, refs.fag_s, refs.fag_r), (exy, refs.exy_s, refs.exy_r)
    ):
        others(buffer, send, recv, plane_peer(1)).wait_send()
    others(zl, refs.zl_s, refs.zl_r, z_peer(1), 4).wait_send()
    raw.drain()
    late.drain()


def call(cap, snapshots, partner_slot):
    rows = snapshots.shape[0]
    raw_rows = RAW_ROWS[cap]
    dma = pltpu.SemaphoreType.DMA
    f32 = lambda *shape: pltpu.VMEM(shape, F32)
    b16 = lambda *shape: pltpu.VMEM(shape, BF16)
    scratch = dict(
        own=f32(2, rows, 2 * BW), xh=b16(2, rows, 2 * BW), xl=b16(2, rows, 2 * BW),
        rh=b16(2, 2, 2 * BW, BW), rl=b16(2, 2, 2 * BW, BW),
        rights=f32(2, rows - raw_rows, BW),
        gmine=f32(XY, 40, 128), gsend=f32(XY, 40, 128), gpeer=f32(XY, 40, 128), rs=f32(XY, 40, 128),
        zsend=f32(40, 128), zrecv=f32(40, 128), ag=f32(XY, 32, 128),
        zl=f32(4, 40, 128), fp=f32(2, 4, 40, 128), fag=f32(XY, 32, 128),
        rsend=f32(3, BW, BW), rrecv=f32(3, BW, BW),
        fsend=f32(2, BW, BW), frecv=f32(2, BW, BW), fh=b16(2, 2 * BW, BW), fl=b16(2, 2 * BW, BW),
        esend=f32(2, 8, 128), epeer=f32(2, 8, 128), exy=f32(XY, 2, 8, 128), ez=f32(2, 2, 8, 128),
        slots=pltpu.SMEM((8,), jnp.int32), ps_sem=dma, load_sem=dma((2,)), pair_s=dma, pair_r=dma, rs_s=dma, rs_r=dma,
        z_s=dma, z_r=dma, ag_s=dma, ag_r=dma, zl_s=dma, zl_r=dma,
        fp_s=dma, fp_r=dma, fag_s=dma, fag_r=dma, ro_s=dma((2,)), ro_r=dma((2,)), f_s=dma, f_r=dma,
        e_s=dma((2,)), e_r=dma((2,)), exy_s=dma, exy_r=dma,
        raw_fin=f32(2, raw_rows, 2 * BW),
    )
    for name, height, width, chunk in (
        ("raw", raw_rows, 2 * BW, RAW_CHUNK), ("late", rows - raw_rows, BW, LATE_CHUNK)
    ):
        for buffer, blocks in (("mid_stage", cap), ("from_mid", cap), ("out_stage", 2), ("from_outer", 2), ("from_inner", 2)):
            scratch[f"{name}_{buffer}"] = f32(blocks, height, width)
        for sem in ("in_s", "mid_s", "out_s"):
            scratch[f"{name}_{sem}"] = dma
        for sem in ("in_r", "mid_r", "out_r"):
            scratch[f"{name}_{sem}"] = dma((height // chunk,))
    scratch["raw_out_r"] = dma
    return pl.pallas_call(
        functools.partial(kernel, cap, tuple(scratch)),
        out_shape=(
            jax.ShapeDtypeStruct(snapshots.shape, F32),
            jax.ShapeDtypeStruct((8, 128), F32),
        ),
        in_specs=[pl.BlockSpec(memory_space=pl.ANY)] * 2,
        out_specs=(pl.BlockSpec(memory_space=pltpu.VMEM), pl.BlockSpec(memory_space=pltpu.VMEM)),
        scratch_shapes=list(scratch.values()),
        name=f"round_{cap}",
        compiler_params=pltpu.CompilerParams(
            collective_id=cap, has_side_effects=True, vmem_limit_bytes=48 << 20
        ),
    )(snapshots, partner_slot)


def hand_out(moved_ref, energies_ref, out_ref, en_ref, sems):
    rows = moved_ref.shape[0] // 4
    copies = [pltpu.make_async_copy(energies_ref, en_ref, sems.at[4])]
    for part in range(4):
        where = pl.ds(part * rows, rows)
        copies.append(pltpu.make_async_copy(moved_ref.at[where], out_ref.at[where], sems.at[part]))
    for copy in copies:
        copy.start()
    for copy in copies:
        copy.wait()


def on_device(snapshots, partner_slot):
    crossing = jnp.sum((partner_slot[:4] >= 4).astype(jnp.int32))
    moved, energies = lax.switch(
        jnp.maximum(crossing, 2) - 2,
        [functools.partial(call, cap) for cap in (2, 3, 4)],
        snapshots,
        partner_slot,
    )
    anywhere = pl.BlockSpec(memory_space=pl.ANY)
    moved, energies = pl.pallas_call(
        hand_out,
        out_shape=(
            jax.ShapeDtypeStruct(moved.shape, F32),
            jax.ShapeDtypeStruct(energies.shape, F32),
        ),
        in_specs=[anywhere, anywhere],
        out_specs=(anywhere, anywhere),
        scratch_shapes=[pltpu.SemaphoreType.DMA((5,))],
        name="hand_out",
    )(moved, energies)
    return moved, energies.reshape(-1)


def solution(mesh):
    in_specs = (P("rows", "cols"), P())
    out_specs = (P("rows", "cols"), P("cols"))
    return jax.shard_map(
        on_device, mesh=mesh, in_specs=in_specs, out_specs=out_specs, check_vma=False
    )
```

```python
import functools
import types

import jax
import jax.numpy as jnp
from jax import lax
from jax.experimental import pallas as pl
from jax.experimental.pallas import tpu as pltpu
from jax.sharding import PartitionSpec as P

BW = 256
SWEEPS = 4
MESH = pl.DeviceIdType.MESH
F32 = jnp.float32
BF16 = jnp.bfloat16
XY = 16
RAW_CHUNK = 16
LATE_CHUNK = 16
EARLY = 6
RAW_FIRST = {2: 4, 3: 3, 4: 2}
RAW_SENT = {2: 7, 3: 5, 4: 4}
RAW_ROWS = {2: 208, 3: 144, 4: 128}


def split(value):
    high = value.astype(BF16)
    return high, (value - high.astype(F32)).astype(BF16)


def dot(left, right, contract=((1,), (0,))):
    return lax.dot_general(left, right, (contract, ((), ())), preferred_element_type=F32)


def dot3(left, right, contract=((1,), (0,))):
    return dot(left[0], right[0], contract) + (
        dot(left[0], right[1], contract) + dot(left[1], right[0], contract)
    )


def coupling_of(pieces, diag_tile):
    cross = jnp.concatenate(
        [pieces[:, 0:16, :].reshape(BW, 128), pieces[:, 16:32, :].reshape(BW, 128)], 1
    )
    left_cols = []
    right_rows = []
    for half in range(2):
        left_row = jnp.broadcast_to(diag_tile[half : half + 1, :], (128, 128))
        left_cols.append(jnp.transpose(left_row))
        right_rows.append(diag_tile[2 + half : 3 + half, :])
    left = jnp.concatenate([jnp.concatenate([part, part], 1) for part in left_cols], 0)
    right = jnp.broadcast_to(jnp.concatenate(right_rows, 1), (BW, BW))
    gap = right - left
    coupling = cross * gap / (gap * gap + 4.0 * cross * cross + 0.25 * left * right)
    scale = lax.rsqrt(jnp.full((1, 1), 1.0, F32) + 2.0 * jnp.sum(coupling * coupling))
    return coupling, scale


def polynomials(starts, scale, between):
    eye = (
        lax.broadcasted_iota(jnp.int32, (BW, BW), 0) == lax.broadcasted_iota(jnp.int32, (BW, BW), 1)
    ).astype(F32)

    def times(uppers, lowers, rights):
        stacks = [jnp.concatenate(parts, 0) for parts in zip(uppers, lowers)]
        results = [dot3(split(stack), split(right)) for stack, right in zip(stacks, rights)]
        return [result[:BW] for result in results], [result[BW:] for result in results]

    firsts = [(eye + start) * (scale * scale) for start in starts]
    parts = [split(first) for first in firsts]
    powers = [dot3(part, part) for part in parts]
    squares, crossed = times(
        [0.25 * first - 1.5 * eye for first in firsts],
        [1.125 * first - 0.125 * power for first, power in zip(firsts, powers)],
        powers,
    )
    squares = [square + 2.25 * first for square, first in zip(squares, firsts)]
    totals = [
        scale * (2.25 * eye - 2.4375 * first + 1.6875 * power - 0.5 * cross)
        for first, power, cross in zip(firsts, powers, crossed)
    ]
    for sweep in range(2, SWEEPS):
        between(2 * sweep - 4)
        powers, crossed = times(squares, totals, squares)
        factors = [2.25 * eye - 1.5 * square + 0.25 * power for square, power in zip(squares, powers)]
        if sweep < SWEEPS - 1:
            between(1)
            squares, crossed = times(squares, crossed, factors)
        else:
            crossed = [dot3(split(cross), split(factor)) for cross, factor in zip(crossed, factors)]
        totals = [1.5 * total - 0.5 * cross for total, cross in zip(totals, crossed)]
    return totals


def pick(options, index):
    value = options[0]
    for position in range(1, len(options)):
        value = jnp.where(index == position, options[position], value)
    return value


def remote(src, dst, send, recv, device):
    return pltpu.make_async_remote_copy(
        src_ref=src, dst_ref=dst, send_sem=send, recv_sem=recv, device_id=device, device_id_type=MESH
    )


def row_of(values):
    return jnp.concatenate(
        [values[:, 128 * part : 128 * (part + 1)] for part in range(4)] + [jnp.zeros((4, 128), F32)], 0
    )


class Stream:
    def __init__(self, whole, near, first, count, chunk, refs, routes, put, fin_first, place):
        self.whole = whole
        self.forwards = self.backs = 0
        self.near, self.first, self.count, self.chunk, self.refs = near, first, count, chunk, refs
        self.routes, self.put, self.fin_first, self.place = routes, put, fin_first, place

    def rows(self, index, offset=0):
        return pl.ds(pl.multiple_of(offset + index * self.chunk, self.chunk), self.chunk)

    def near_rows(self, index):
        return self.rows(index, self.first)

    def in_copy(self, index, device):
        refs = self.refs
        return remote(
            self.near.at[:, self.near_rows(index)], refs.from_outer.at[:, self.rows(index)],
            refs.in_s, refs.in_r.at[index], device,
        )

    def mid_copy(self, index):
        refs = self.refs
        return remote(
            refs.mid_stage.at[:, self.rows(index)], refs.from_mid.at[:, self.rows(index)],
            refs.mid_s, refs.mid_r.at[index], self.place.mid_peer,
        )

    def out_copy(self, index, device):
        refs = self.refs
        return remote(
            refs.out_stage.at[:, self.rows(index)], refs.from_inner.at[:, self.rows(index)],
            refs.out_s, self.out_sem(index), device,
        )

    def out_sem(self, index):
        return self.refs.out_r if self.whole else self.refs.out_r.at[index]

    def near_options(self, index):
        return [self.near[entry, self.near_rows(index), :] for entry in range(2)]

    def forward(self, index):
        self.in_copy(index, self.place.outer_peer).wait_recv()
        rows = self.rows(index)
        refs = self.refs
        options = self.near_options(index) + [refs.from_outer[entry, rows, :] for entry in range(2)]
        for entry in range(refs.mid_stage.shape[0]):
            refs.mid_stage[entry, rows, :] = pick(options, self.routes.mid[entry])
        self.mid_copy(index).start()

    def back(self, index):
        self.mid_copy(index).wait_recv()
        rows = self.rows(index)
        refs = self.refs
        near = self.near_options(index)
        beyond = [refs.from_mid[entry, rows, :] for entry in range(refs.from_mid.shape[0])]
        for entry in range(2):
            refs.out_stage[entry, rows, :] = pick(near + beyond, self.routes.out[entry])
        self.out_copy(index, self.place.outer_peer).start()
        options = near + [refs.from_outer[entry, rows, :] for entry in range(2)] + beyond
        for entry in range(2):
            self.put(entry, self.rows(index, self.fin_first), pick(options, self.routes.inner[entry]))

    def arrive(self, index):
        if not self.whole:
            self.out_copy(index, self.place.inner_peer).wait_recv()
        rows = self.rows(index)
        options = self.near_options(index) + [self.refs.from_inner[entry, rows, :] for entry in range(2)]
        for entry in range(2):
            self.put(entry, self.rows(index, self.fin_first), pick(options, self.routes.outer[entry]))

    def send(self, first, last):
        @pl.when(self.place.is_outer)
        def _():
            @pl.loop(first, last)
            def _(index):
                self.in_copy(index, self.place.inner_peer).start()

    def send_slot(self, slot, first, last):
        refs = self.refs

        @pl.when(self.place.is_outer)
        def _():
            @pl.loop(first, last)
            def _(index):
                remote(
                    self.near.at[slot, self.near_rows(index)], refs.from_outer.at[slot, self.rows(index)],
                    refs.in_s, refs.in_r.at[index], self.place.inner_peer,
                ).start()

    def go(self, forwards, backs):
        forwards = max(self.forwards, min(forwards, self.count))
        backs = max(self.backs, min(backs, forwards))

        @pl.when(self.place.is_inner)
        def _():
            pl.loop(self.forwards, forwards)(self.forward)
            pl.loop(self.backs, backs)(self.back)

        self.forwards, self.backs = forwards, backs

    def finish(self):
        ahead = self.forwards - self.backs
        first, last = self.backs, self.count - ahead

        @pl.when(self.place.is_inner)
        def _():
            @pl.loop(first, last)
            def _(index):
                self.back(index)
                self.forward(index + ahead)

        self.forwards, self.backs = self.count, last
        self.go(self.count, self.count)

    def arrivals(self):
        @pl.when(self.place.is_outer)
        def _():
            if self.whole:
                refs = self.refs
                remote(
                    refs.out_stage, refs.from_inner, refs.out_s, refs.out_r, self.place.inner_peer
                ).wait_recv()
            pl.loop(0, self.count)(self.arrive)

    def drain(self):
        refs, place = self.refs, self.place

        @pl.when(place.is_outer)
        def _():
            sent = self.near.at[:, pl.ds(self.first, self.count * self.chunk)]
            remote(sent, refs.from_outer, refs.in_s, refs.in_r.at[0], place.inner_peer).wait_send()

        @pl.when(place.is_inner)
        def _():
            remote(refs.mid_stage, refs.from_mid, refs.mid_s, refs.mid_r.at[0], place.mid_peer).wait_send()
            remote(
                refs.out_stage, refs.from_inner, refs.out_s, self.out_sem(0), place.outer_peer
            ).wait_send()


def routes_of(ps_ref, side, cap):
    slots = []
    for first, second in zip((2, 3, 0, 1, 4, 5, 6, 7), (4, 5, 6, 7, 2, 3, 0, 1)):
        slot = ps_ref[first + side * (second - first)]
        low_side = jnp.where(slot < 2, slot + 2, jnp.where(slot < 4, slot - 2, slot))
        high_side = jnp.where(slot < 2, slot + 6, jnp.where(slot < 4, slot + 2, slot - 4))
        slots.append(jnp.where(side == 0, low_side, high_side))
    crosses = lambda slot: slot >= 4
    returns = lambda slot: slot < 4
    outward = lambda slot: (slot == 2) | (slot == 3)

    def ranks(order, wanted):
        count = jnp.int32(0)
        result = {}
        for position in order:
            result[position] = count
            count = count + jnp.where(wanted(slots[position]), 1, 0)
        return result

    def source_of(places, wanted):
        found = jnp.int32(0)
        for position, place in places.items():
            found = jnp.where(wanted(position), place, found)
        return found

    send_rank = ranks((0, 1, 2, 3), crosses)
    recv_rank = ranks((4, 5, 6, 7), returns)
    out_rank = ranks((0, 1, 4, 5, 6, 7), outward)
    far_places = {position: recv_rank[position] for position in (4, 5, 6, 7)}
    mid_places = {position: position for position in range(4)}
    out_places = {0: 0, 1: 1, **{position: 2 + place for position, place in far_places.items()}}
    inner_places = {**mid_places, **{position: 4 + place for position, place in far_places.items()}}
    outer_places = {2: 0, 3: 1, **{position: 2 + rank for position, rank in out_rank.items()}}
    return types.SimpleNamespace(
        mid=[
            source_of(mid_places, lambda p: crosses(slots[p]) & (send_rank[p] == entry))
            for entry in range(cap)
        ],
        out=[
            source_of(out_places, lambda p: outward(slots[p]) & (out_rank[p] == entry))
            for entry in range(2)
        ],
        inner=[source_of(inner_places, lambda p: slots[p] == entry) for entry in range(2)],
        outer=[source_of(outer_places, lambda p: slots[p] == 2 + entry) for entry in range(2)],
    )


def kernel(cap, names, x_hbm, ps_any, out_ref, en_ref, *scratch):
    refs = types.SimpleNamespace(**dict(zip(names, scratch)))
    own, xh, xl, rh, rl = refs.own, refs.xh, refs.xl, refs.rh, refs.rl
    rows_here = own.shape[1]
    raw_rows = refs.raw_fin.shape[1]
    row = lax.axis_index("rows")
    z = lax.axis_index("cols")
    core = row % 2
    xy = (row // 2) % XY
    zh = row // (2 * XY)
    side = z // 2
    place = types.SimpleNamespace(
        is_outer=(z % 3) == 0,
        is_inner=(z % 3) != 0,
        inner_peer={"cols": 1 + z // 3},
        outer_peer={"cols": (3 * z + 1) % 4},
        mid_peer={"cols": 3 - z},
    )
    sibling = {"rows": row + 1 - 2 * core}
    far = {"rows": (row + 2 * XY) % (4 * XY)}

    def plane_peer(step):
        return {"rows": zh * 2 * XY + ((xy + step) % XY) * 2 + core}

    def z_peer(step):
        return {"cols": (z + step) % 4}

    def greet(device):
        pl.semaphore_signal(barrier, inc=1, device_id=device, device_id_type=MESH)

    def load(pair):
        where = pl.ds(pl.multiple_of(pair * 2 * BW, 2 * BW), 2 * BW)
        return pltpu.make_async_copy(x_hbm.at[:, where], own.at[pair], refs.load_sem.at[pair])

    load(1 - core).start()
    load(core).start()
    ps_ref = refs.slots
    ps_load = pltpu.make_async_copy(ps_any, ps_ref, refs.ps_sem)
    ps_load.start()
    barrier = pltpu.get_barrier_semaphore()
    greet(sibling)
    greet(far)

    @pl.loop(1, XY)
    def _(step):
        greet(plane_peer(step))

    @pl.loop(1, 4)
    def _(step):
        greet(z_peer(step))

    routes = types.SimpleNamespace()
    raw_refs = types.SimpleNamespace(**{n[4:]: r for n, r in vars(refs).items() if n.startswith("raw_")})
    late_refs = types.SimpleNamespace(**{n[5:]: r for n, r in vars(refs).items() if n.startswith("late_")})
    raw_count = raw_rows // RAW_CHUNK
    late_count = (rows_here - raw_rows) // LATE_CHUNK
    def column(pair, half):
        return pl.ds(pl.multiple_of(pair * 2 * BW + half * BW, BW), BW)

    def put_raw(entry, rows, value):
        refs.raw_fin[entry, rows, :] = value

    def put_late(entry, rows, value):
        out_ref[rows, column(entry, 1)] = value

    raw = Stream(True, own, 0, raw_count, RAW_CHUNK, raw_refs, routes, put_raw, 0, place)
    late = Stream(False, refs.rights, 0, late_count, LATE_CHUNK, late_refs, routes, put_late, raw_rows, place)
    first_batch = RAW_FIRST[cap]
    first_sent = RAW_SENT[cap]

    def go_raw(forwards, backs):
        raw.go(first_batch + forwards * 2 // cap, first_batch + backs * 2 // cap)

    def go_late(forwards, backs):
        late.go(forwards * 2 // cap, backs * 2 // cap)

    def gram(pair, target):
        load(pair).wait()
        high, low = split(own[pair])
        xh[pair] = high
        xl[pair] = low
        rows = ((0,), (0,))
        cross = dot3((high[:, :BW], low[:, :BW]), (high[:, BW:], low[:, BW:]), rows)
        target[:, 0:16, :] = cross[:, :128].reshape(XY, 16, 128)
        target[:, 16:32, :] = cross[:, 128:].reshape(XY, 16, 128)
        values = own[pair]
        tile = row_of(jnp.sum(values * values, axis=0, keepdims=True))
        target[:, 32:40, :] = jnp.broadcast_to(tile[None], (XY, 8, 128))

    gmine, gsend, gpeer, rs = refs.gmine, refs.gsend, refs.gpeer, refs.rs
    gram(1 - core, gsend)
    gram(core, gmine)
    pl.semaphore_wait(barrier, 20)
    to_sibling = remote(gsend, gpeer, refs.pair_s, refs.pair_r, sibling)
    to_sibling.start()

    raw.send(0, first_sent)
    to_sibling.wait_recv()
    gmine[...] = gmine[...] + gpeer[...]

    def rs_copy(step):
        target = (xy + step) % XY
        return remote(gmine.at[target], rs.at[xy], refs.rs_s, refs.rs_r, plane_peer(step))

    def gather_copy(buffer, send, recv):
        return lambda step: remote(buffer.at[xy], buffer.at[xy], send, recv, plane_peer(step))

    def start_all(copy, last=XY):
        @pl.loop(1, last)
        def _(step):
            copy(step).start()

    def others(buffer, send, recv, device, last=XY):
        part = buffer.at[pl.ds(0, last - 1)]
        return remote(part, part, send, recv, device)

    start_all(rs_copy)
    rs[xy] = gmine[xy]

    ps_load.wait()
    vars(routes).update(vars(routes_of(ps_ref, side, cap)))
    raw.go(first_batch, 0)
    others(rs, refs.rs_s, refs.rs_r, plane_peer(1)).wait_recv()
    total = rs[0]
    for chip in range(1, XY):
        total = total + rs[chip]
    refs.zsend[...] = total
    to_far = remote(refs.zsend, refs.zrecv, refs.z_s, refs.z_r, far)
    to_far.start()
    to_far.wait_recv()
    total = refs.zsend[...] + refs.zrecv[...]
    diag_tile = total[32:40, :]
    ag, zl, fp, fag = refs.ag, refs.zl, refs.fp, refs.fag
    ag[xy] = total[0:32, :]
    zl[z] = total
    ag_copy = gather_copy(ag, refs.ag_s, refs.ag_r)
    start_all(ag_copy)

    def zl_copy(step):
        return remote(zl.at[z], zl.at[z], refs.zl_s, refs.zl_r, z_peer(step))

    start_all(zl_copy, 4)
    raw.send(first_sent, raw_count)
    go_raw(2, 0)
    go_raw(3, 1)
    others(ag, refs.ag_s, refs.ag_r, plane_peer(1)).wait_recv()

    coupling, scale = coupling_of(ag[...], diag_tile)
    go_raw(4, 2)
    rsend, rrecv = refs.rsend, refs.rrecv
    rsend[0] = coupling
    to_sibling_k = remote(rsend.at[0], rrecv.at[0], refs.ro_s.at[2], refs.ro_r.at[2], sibling)
    to_sibling_k.start()
    coupling_parts = split(coupling)
    outer_product = dot3(coupling_parts, coupling_parts, ((1,), (1,)))
    inner_product = dot3(coupling_parts, coupling_parts, ((0,), (0,)))
    others(zl, refs.zl_s, refs.zl_r, z_peer(1), 4).wait_recv()
    fp[core] = zl[...]
    to_sibling_z = remote(zl, fp.at[core], refs.fp_s, refs.fp_r, sibling)
    to_sibling_z.start()
    fag_copy = gather_copy(fag, refs.fag_s, refs.fag_r)
    incoming_diag = []

    def gather_incoming():
        remote(zl, fp.at[1 - core], refs.fp_s, refs.fp_r, sibling).wait_recv()
        parity, plane = jnp.int32(0), jnp.int32(0)
        for pair in range(8):
            hit = ps_ref[pair] == 2 * z + core
            parity = jnp.where(hit, pair % 2, parity)
            plane = jnp.where(hit, pair // 2, plane)
        incoming = fp[parity, plane]
        fag[xy] = incoming[0:32, :]
        incoming_diag.append(incoming[32:40, :])
        start_all(fag_copy)

    def beside(sweep):
        go_raw(*((5, 3), (6, 3), (7, 4))[sweep])

    go_raw(5, 2)
    left_part, right_part = polynomials(
        [outer_product, inner_product], scale, beside
    )
    rsend[1] = right_part
    to_sibling_r = remote(rsend.at[1], rrecv.at[1], refs.ro_s.at[0], refs.ro_r.at[0], sibling)
    to_sibling_r.start()
    rsend[2] = left_part
    to_sibling_l = remote(rsend.at[2], rrecv.at[2], refs.ro_s.at[1], refs.ro_r.at[1], sibling)
    to_sibling_l.start()

    def spread(half, pair, blocks):
        for row_block, block in enumerate(blocks):
            high, low = split(block)
            where = (half, pair, pl.ds(row_block * BW, BW))
            rh[where] = high
            rl[where] = low

    rights = refs.rights
    esend, epeer, exy, ez = refs.esend, refs.epeer, refs.exy, refs.ez

    def rotate(half, pair, first, last):
        rows = pl.ds(first, last - first)
        result = dot3((xh[pair, rows, :], xl[pair, rows, :]), (rh[half, pair], rl[half, pair]))
        if half == 0:
            out_ref[rows, column(pair, 0)] = result
        elif first > 0:
            rights[pair] = result
        return jnp.sum(result * result, axis=0, keepdims=True)

    def across_of(source, entry):
        return dot3(split(source[0]), split(source[entry]))

    acrosses = [across_of(rsend, 1)]
    spread(1, core, (acrosses[0], right_part))
    right_sums = [rotate(1, core, raw_rows, rows_here)]
    late.send_slot(core, 0, EARLY)
    go_raw(9, 5)
    gather_incoming()
    go_raw(10, 6)
    to_sibling_k.wait_recv()
    to_sibling_r.wait_recv()
    acrosses.append(across_of(rrecv, 1))
    spread(1, 1 - core, (acrosses[1], rrecv[1]))
    right_sums.append(rotate(1, 1 - core, raw_rows, rows_here))

    late.send_slot(1 - core, 0, EARLY)
    late.send(EARLY, late_count)
    go_raw(raw_count, 7)
    to_sibling_l.wait_recv()
    left_sums = []

    def rotate_left(pair, source):
        spread(0, pair, (source[2], -jnp.transpose(acrosses[len(left_sums)])))
        left_sums.append(rotate(0, pair, 0, rows_here))

    rotate_left(core, rsend)
    go_raw(raw_count, 8)
    rotate_left(1 - core, rrecv)
    go_raw(raw_count, 9)
    go_late(1, 0)
    for entry, pair in enumerate((core, 1 - core)):
        sums = right_sums[entry] + rotate(1, pair, 0, raw_rows)
        esend[pair] = row_of(jnp.concatenate([left_sums[entry], sums], 1))
    e_sibling = remote(esend, epeer, refs.e_s.at[0], refs.e_r.at[0], sibling)
    e_sibling.start()
    go_raw(raw_count, 9)
    go_late(3, 0)
    raw.go(raw_count, raw_count)

    others(fag, refs.fag_s, refs.fag_r, plane_peer(1)).wait_recv()
    fsend, frecv, fh, fl = refs.fsend, refs.frecv, refs.fh, refs.fl
    coupling, scale = coupling_of(fag[...], incoming_diag[0])
    coupling_parts = split(coupling)
    go_late(5, 0)
    inner_product = dot3(coupling_parts, coupling_parts, ((0,), (0,)))
    e_sibling.wait_recv()
    exy[xy] = esend[...] + epeer[...]
    exy_copy = gather_copy(exy, refs.exy_s, refs.exy_r)
    start_all(exy_copy)
    go_late(8, 1)
    (right_part,) = polynomials(
        [inner_product], scale, lambda sweep: go_late(*((9, 2), (11, 3), (12, 5))[sweep])
    )
    fsend[1] = right_part
    fsend[0] = dot3(coupling_parts, split(right_part))
    to_sibling_f = remote(fsend, frecv, refs.f_s, refs.f_r, sibling)
    to_sibling_f.start()
    raw.arrivals()
    go_late(14, 7)
    others(exy, refs.exy_s, refs.exy_r, plane_peer(1)).wait_recv()
    plane_sum = exy[0]
    for chip in range(1, XY):
        plane_sum = plane_sum + exy[chip]
    ez[0] = plane_sum
    e_far = remote(ez.at[0], ez.at[1], refs.e_s.at[1], refs.e_r.at[1], far)
    e_far.start()

    def finish_raw(slot, source):
        for block in range(2):
            high, low = split(source[block])
            fh[slot, pl.ds(block * BW, BW), :] = high
            fl[slot, pl.ds(block * BW, BW), :] = low
        out_ref[pl.ds(0, raw_rows), column(slot, 1)] = dot3(split(refs.raw_fin[slot]), (fh[slot], fl[slot]))

    finish_raw(core, fsend)
    go_late(16, 9)
    to_sibling_f.wait_recv()
    finish_raw(1 - core, frecv)
    late.finish()
    late.arrivals()
    e_far.wait_recv()
    energies = (ez[0] + ez[1]) / (4 * XY * rows_here)
    en_ref[0:4, :] = energies[0, 0:4, :]
    en_ref[4:8, :] = energies[1, 0:4, :]

    for copy in (to_sibling, to_sibling_k, to_sibling_r, to_sibling_l, to_sibling_z, to_sibling_f, to_far, e_sibling, e_far):
        copy.wait_send()

    for buffer, send, recv in (
        (rs, refs.rs_s, refs.rs_r), (ag, refs.ag_s, refs.ag_r), (fag, refs.fag_s, refs.fag_r), (exy, refs.exy_s, refs.exy_r)
    ):
        others(buffer, send, recv, plane_peer(1)).wait_send()
    others(zl, refs.zl_s, refs.zl_r, z_peer(1), 4).wait_send()
    raw.drain()
    late.drain()


def call(cap, snapshots, partner_slot):
    rows = snapshots.shape[0]
    raw_rows = RAW_ROWS[cap]
    dma = pltpu.SemaphoreType.DMA
    f32 = lambda *shape: pltpu.VMEM(shape, F32)
    b16 = lambda *shape: pltpu.VMEM(shape, BF16)
    scratch = dict(
        own=f32(2, rows, 2 * BW), xh=b16(2, rows, 2 * BW), xl=b16(2, rows, 2 * BW),
        rh=b16(2, 2, 2 * BW, BW), rl=b16(2, 2, 2 * BW, BW),
        rights=f32(2, rows - raw_rows, BW),
        gmine=f32(XY, 40, 128), gsend=f32(XY, 40, 128), gpeer=f32(XY, 40, 128), rs=f32(XY, 40, 128),
        zsend=f32(40, 128), zrecv=f32(40, 128), ag=f32(XY, 32, 128),
        zl=f32(4, 40, 128), fp=f32(2, 4, 40, 128), fag=f32(XY, 32, 128),
        rsend=f32(3, BW, BW), rrecv=f32(3, BW, BW),
        fsend=f32(2, BW, BW), frecv=f32(2, BW, BW), fh=b16(2, 2 * BW, BW), fl=b16(2, 2 * BW, BW),
        esend=f32(2, 8, 128), epeer=f32(2, 8, 128), exy=f32(XY, 2, 8, 128), ez=f32(2, 2, 8, 128),
        slots=pltpu.SMEM((8,), jnp.int32), ps_sem=dma, load_sem=dma((2,)), pair_s=dma, pair_r=dma, rs_s=dma, rs_r=dma,
        z_s=dma, z_r=dma, ag_s=dma, ag_r=dma, zl_s=dma, zl_r=dma,
        fp_s=dma, fp_r=dma, fag_s=dma, fag_r=dma, ro_s=dma((3,)), ro_r=dma((3,)), f_s=dma, f_r=dma,
        e_s=dma((2,)), e_r=dma((2,)), exy_s=dma, exy_r=dma,
        raw_fin=f32(2, raw_rows, 2 * BW),
    )
    for name, height, width, chunk in (
        ("raw", raw_rows, 2 * BW, RAW_CHUNK), ("late", rows - raw_rows, BW, LATE_CHUNK)
    ):
        for buffer, blocks in (("mid_stage", cap), ("from_mid", cap), ("out_stage", 2), ("from_outer", 2), ("from_inner", 2)):
            scratch[f"{name}_{buffer}"] = f32(blocks, height, width)
        for sem in ("in_s", "mid_s", "out_s"):
            scratch[f"{name}_{sem}"] = dma
        for sem in ("in_r", "mid_r", "out_r"):
            scratch[f"{name}_{sem}"] = dma((height // chunk,))
    scratch["raw_out_r"] = dma
    return pl.pallas_call(
        functools.partial(kernel, cap, tuple(scratch)),
        out_shape=(
            jax.ShapeDtypeStruct(snapshots.shape, F32),
            jax.ShapeDtypeStruct((8, 128), F32),
        ),
        in_specs=[pl.BlockSpec(memory_space=pl.ANY)] * 2,
        out_specs=(pl.BlockSpec(memory_space=pltpu.VMEM), pl.BlockSpec(memory_space=pltpu.VMEM)),
        scratch_shapes=list(scratch.values()),
        name=f"round_{cap}",
        compiler_params=pltpu.CompilerParams(
            collective_id=cap, has_side_effects=True, vmem_limit_bytes=48 << 20
        ),
    )(snapshots, partner_slot)


def hand_out(moved_ref, energies_ref, out_ref, en_ref, sems):
    rows = moved_ref.shape[0] // 4
    copies = [pltpu.make_async_copy(energies_ref, en_ref, sems.at[4])]
    for part in range(4):
        where = pl.ds(part * rows, rows)
        copies.append(pltpu.make_async_copy(moved_ref.at[where], out_ref.at[where], sems.at[part]))
    for copy in copies:
        copy.start()
    for copy in copies:
        copy.wait()


def on_device(snapshots, partner_slot):
    crossing = jnp.sum((partner_slot[:4] >= 4).astype(jnp.int32))
    moved, energies = lax.switch(
        jnp.maximum(crossing, 2) - 2,
        [functools.partial(call, cap) for cap in (2, 3, 4)],
        snapshots,
        partner_slot,
    )
    anywhere = pl.BlockSpec(memory_space=pl.ANY)
    moved, energies = pl.pallas_call(
        hand_out,
        out_shape=(
            jax.ShapeDtypeStruct(moved.shape, F32),
            jax.ShapeDtypeStruct(energies.shape, F32),
        ),
        in_specs=[anywhere, anywhere],
        out_specs=(anywhere, anywhere),
        scratch_shapes=[pltpu.SemaphoreType.DMA((5,))],
        name="hand_out",
    )(moved, energies)
    return moved, energies.reshape(-1)


def solution(mesh):
    in_specs = (P("rows", "cols"), P())
    out_specs = (P("rows", "cols"), P("cols"))
    return jax.shard_map(
        on_device, mesh=mesh, in_specs=in_specs, out_specs=out_specs, check_vma=False
    )
```

```python
import functools
import types

import jax
import jax.numpy as jnp
from jax import lax
from jax.experimental import pallas as pl
from jax.experimental.pallas import tpu as pltpu
from jax.sharding import PartitionSpec as P

BW = 256
SWEEPS = 4
MESH = pl.DeviceIdType.MESH
F32 = jnp.float32
BF16 = jnp.bfloat16
XY = 16
RAW_CHUNK = 16
LATE_CHUNK = 16
EARLY = 6
RAW_FIRST = {2: 4, 3: 3, 4: 2}
RAW_SENT = {2: 6, 3: 5, 4: 4}
RAW_BACK = {2: 3, 3: 1, 4: 1}
RAW_ROWS = {2: 208, 3: 144, 4: 128}


def split(value):
    high = value.astype(BF16)
    return high, (value - high.astype(F32)).astype(BF16)


def dot(left, right, contract=((1,), (0,))):
    return lax.dot_general(left, right, (contract, ((), ())), preferred_element_type=F32)


def dot3(left, right, contract=((1,), (0,))):
    return dot(left[0], right[0], contract) + (
        dot(left[0], right[1], contract) + dot(left[1], right[0], contract)
    )


def coupling_of(pieces, diag_tile):
    cross = jnp.concatenate(
        [pieces[:, 0:16, :].reshape(BW, 128), pieces[:, 16:32, :].reshape(BW, 128)], 1
    )
    left_cols = []
    right_rows = []
    for half in range(2):
        left_row = jnp.broadcast_to(diag_tile[half : half + 1, :], (128, 128))
        left_cols.append(jnp.transpose(left_row))
        right_rows.append(diag_tile[2 + half : 3 + half, :])
    left = jnp.concatenate([jnp.concatenate([part, part], 1) for part in left_cols], 0)
    right = jnp.broadcast_to(jnp.concatenate(right_rows, 1), (BW, BW))
    gap = right - left
    coupling = cross * gap / (gap * gap + 4.0 * cross * cross + 0.25 * left * right)
    scale = lax.rsqrt(jnp.full((1, 1), 1.0, F32) + 2.0 * jnp.sum(coupling * coupling))
    return coupling, scale


def polynomials(starts, scale, between):
    eye = (
        lax.broadcasted_iota(jnp.int32, (BW, BW), 0) == lax.broadcasted_iota(jnp.int32, (BW, BW), 1)
    ).astype(F32)

    def times(uppers, lowers, rights):
        stacks = [jnp.concatenate(parts, 0) for parts in zip(uppers, lowers)]
        results = [dot3(split(stack), split(right)) for stack, right in zip(stacks, rights)]
        return [result[:BW] for result in results], [result[BW:] for result in results]

    firsts = [(eye + start) * (scale * scale) for start in starts]
    parts = [split(first) for first in firsts]
    powers = [dot3(part, part) for part in parts]
    squares, crossed = times(
        [0.25 * first - 1.5 * eye for first in firsts],
        [1.125 * first - 0.125 * power for first, power in zip(firsts, powers)],
        powers,
    )
    squares = [square + 2.25 * first for square, first in zip(squares, firsts)]
    totals = [
        scale * (2.25 * eye - 2.4375 * first + 1.6875 * power - 0.5 * cross)
        for first, power, cross in zip(firsts, powers, crossed)
    ]
    for sweep in range(2, SWEEPS):
        between(2 * sweep - 4)
        powers, crossed = times(squares, totals, squares)
        factors = [2.25 * eye - 1.5 * square + 0.25 * power for square, power in zip(squares, powers)]
        if sweep < SWEEPS - 1:
            between(1)
            squares, crossed = times(squares, crossed, factors)
        else:
            crossed = [dot3(split(cross), split(factor)) for cross, factor in zip(crossed, factors)]
        totals = [1.5 * total - 0.5 * cross for total, cross in zip(totals, crossed)]
    return totals


def pick(options, index):
    value = options[0]
    for position in range(1, len(options)):
        value = jnp.where(index == position, options[position], value)
    return value


def remote(src, dst, send, recv, device):
    return pltpu.make_async_remote_copy(
        src_ref=src, dst_ref=dst, send_sem=send, recv_sem=recv, device_id=device, device_id_type=MESH
    )


def row_of(values):
    return jnp.concatenate(
        [values[:, 128 * part : 128 * (part + 1)] for part in range(4)] + [jnp.zeros((4, 128), F32)], 0
    )


class Stream:
    def __init__(self, whole, near, first, count, chunk, refs, routes, put, fin_first, place):
        self.whole = whole
        self.forwards = self.backs = 0
        self.near, self.first, self.count, self.chunk, self.refs = near, first, count, chunk, refs
        self.routes, self.put, self.fin_first, self.place = routes, put, fin_first, place

    def rows(self, index, offset=0):
        return pl.ds(pl.multiple_of(offset + index * self.chunk, self.chunk), self.chunk)

    def near_rows(self, index):
        return self.rows(index, self.first)

    def in_copy(self, index, device):
        refs = self.refs
        return remote(
            self.near.at[:, self.near_rows(index)], refs.from_outer.at[:, self.rows(index)],
            refs.in_s, refs.in_r.at[index], device,
        )

    def mid_copy(self, index):
        refs = self.refs
        return remote(
            refs.mid_stage.at[:, self.rows(index)], refs.from_mid.at[:, self.rows(index)],
            refs.mid_s, refs.mid_r.at[index], self.place.mid_peer,
        )

    def out_copy(self, index, device):
        refs = self.refs
        return remote(
            refs.out_stage.at[:, self.rows(index)], refs.from_inner.at[:, self.rows(index)],
            refs.out_s, self.out_sem(index), device,
        )

    def out_sem(self, index):
        return self.refs.out_r if self.whole else self.refs.out_r.at[index]

    def near_options(self, index):
        return [self.near[entry, self.near_rows(index), :] for entry in range(2)]

    def forward(self, index):
        self.in_copy(index, self.place.outer_peer).wait_recv()
        rows = self.rows(index)
        refs = self.refs
        options = self.near_options(index) + [refs.from_outer[entry, rows, :] for entry in range(2)]
        for entry in range(refs.mid_stage.shape[0]):
            refs.mid_stage[entry, rows, :] = pick(options, self.routes.mid[entry])
        self.mid_copy(index).start()

    def back(self, index):
        self.mid_copy(index).wait_recv()
        rows = self.rows(index)
        refs = self.refs
        near = self.near_options(index)
        beyond = [refs.from_mid[entry, rows, :] for entry in range(refs.from_mid.shape[0])]
        for entry in range(2):
            refs.out_stage[entry, rows, :] = pick(near + beyond, self.routes.out[entry])
        self.out_copy(index, self.place.outer_peer).start()
        options = near + [refs.from_outer[entry, rows, :] for entry in range(2)] + beyond
        for entry in range(2):
            self.put(entry, self.rows(index, self.fin_first), pick(options, self.routes.inner[entry]))

    def arrive(self, index):
        if not self.whole:
            self.out_copy(index, self.place.inner_peer).wait_recv()
        rows = self.rows(index)
        options = self.near_options(index) + [self.refs.from_inner[entry, rows, :] for entry in range(2)]
        for entry in range(2):
            self.put(entry, self.rows(index, self.fin_first), pick(options, self.routes.outer[entry]))

    def send(self, first, last):
        @pl.when(self.place.is_outer)
        def _():
            @pl.loop(first, last)
            def _(index):
                self.in_copy(index, self.place.inner_peer).start()

    def send_slot(self, slot, first, last):
        refs = self.refs

        @pl.when(self.place.is_outer)
        def _():
            @pl.loop(first, last)
            def _(index):
                remote(
                    self.near.at[slot, self.near_rows(index)], refs.from_outer.at[slot, self.rows(index)],
                    refs.in_s, refs.in_r.at[index], self.place.inner_peer,
                ).start()

    def go(self, forwards, backs):
        forwards = max(self.forwards, min(forwards, self.count))
        backs = max(self.backs, min(backs, forwards))

        @pl.when(self.place.is_inner)
        def _():
            pl.loop(self.forwards, forwards)(self.forward)
            pl.loop(self.backs, backs)(self.back)

        self.forwards, self.backs = forwards, backs

    def finish(self):
        ahead = self.forwards - self.backs
        first, last = self.backs, self.count - ahead

        @pl.when(self.place.is_inner)
        def _():
            @pl.loop(first, last)
            def _(index):
                self.back(index)
                self.forward(index + ahead)

        self.forwards, self.backs = self.count, last
        self.go(self.count, self.count)

    def arrivals(self):
        @pl.when(self.place.is_outer)
        def _():
            if self.whole:
                refs = self.refs
                remote(
                    refs.out_stage, refs.from_inner, refs.out_s, refs.out_r, self.place.inner_peer
                ).wait_recv()
            pl.loop(0, self.count)(self.arrive)

    def drain(self):
        refs, place = self.refs, self.place

        @pl.when(place.is_outer)
        def _():
            sent = self.near.at[:, pl.ds(self.first, self.count * self.chunk)]
            remote(sent, refs.from_outer, refs.in_s, refs.in_r.at[0], place.inner_peer).wait_send()

        @pl.when(place.is_inner)
        def _():
            remote(refs.mid_stage, refs.from_mid, refs.mid_s, refs.mid_r.at[0], place.mid_peer).wait_send()
            remote(
                refs.out_stage, refs.from_inner, refs.out_s, self.out_sem(0), place.outer_peer
            ).wait_send()


def routes_of(ps_ref, side, cap):
    slots = []
    for first, second in zip((2, 3, 0, 1, 4, 5, 6, 7), (4, 5, 6, 7, 2, 3, 0, 1)):
        slot = ps_ref[first + side * (second - first)]
        low_side = jnp.where(slot < 2, slot + 2, jnp.where(slot < 4, slot - 2, slot))
        high_side = jnp.where(slot < 2, slot + 6, jnp.where(slot < 4, slot + 2, slot - 4))
        slots.append(jnp.where(side == 0, low_side, high_side))
    crosses = lambda slot: slot >= 4
    returns = lambda slot: slot < 4
    outward = lambda slot: (slot == 2) | (slot == 3)

    def ranks(order, wanted):
        count = jnp.int32(0)
        result = {}
        for position in order:
            result[position] = count
            count = count + jnp.where(wanted(slots[position]), 1, 0)
        return result

    def source_of(places, wanted):
        found = jnp.int32(0)
        for position, place in places.items():
            found = jnp.where(wanted(position), place, found)
        return found

    send_rank = ranks((0, 1, 2, 3), crosses)
    recv_rank = ranks((4, 5, 6, 7), returns)
    out_rank = ranks((0, 1, 4, 5, 6, 7), outward)
    far_places = {position: recv_rank[position] for position in (4, 5, 6, 7)}
    mid_places = {position: position for position in range(4)}
    out_places = {0: 0, 1: 1, **{position: 2 + place for position, place in far_places.items()}}
    inner_places = {**mid_places, **{position: 4 + place for position, place in far_places.items()}}
    outer_places = {2: 0, 3: 1, **{position: 2 + rank for position, rank in out_rank.items()}}
    return types.SimpleNamespace(
        mid=[
            source_of(mid_places, lambda p: crosses(slots[p]) & (send_rank[p] == entry))
            for entry in range(cap)
        ],
        out=[
            source_of(out_places, lambda p: outward(slots[p]) & (out_rank[p] == entry))
            for entry in range(2)
        ],
        inner=[source_of(inner_places, lambda p: slots[p] == entry) for entry in range(2)],
        outer=[source_of(outer_places, lambda p: slots[p] == 2 + entry) for entry in range(2)],
    )


def kernel(cap, names, x_hbm, ps_any, out_ref, en_ref, *scratch):
    refs = types.SimpleNamespace(**dict(zip(names, scratch)))
    own, xh, xl, rh, rl = refs.own, refs.xh, refs.xl, refs.rh, refs.rl
    rows_here = own.shape[1]
    raw_rows = refs.raw_fin.shape[1]
    row = lax.axis_index("rows")
    z = lax.axis_index("cols")
    core = row % 2
    xy = (row // 2) % XY
    zh = row // (2 * XY)
    side = z // 2
    place = types.SimpleNamespace(
        is_outer=(z % 3) == 0,
        is_inner=(z % 3) != 0,
        inner_peer={"cols": 1 + z // 3},
        outer_peer={"cols": (3 * z + 1) % 4},
        mid_peer={"cols": 3 - z},
    )
    sibling = {"rows": row + 1 - 2 * core}
    far = {"rows": (row + 2 * XY) % (4 * XY)}

    def plane_peer(step):
        return {"rows": zh * 2 * XY + ((xy + step) % XY) * 2 + core}

    def z_peer(step):
        return {"cols": (z + step) % 4}

    def greet(device):
        pl.semaphore_signal(barrier, inc=1, device_id=device, device_id_type=MESH)

    def load(pair):
        where = pl.ds(pl.multiple_of(pair * 2 * BW, 2 * BW), 2 * BW)
        return pltpu.make_async_copy(x_hbm.at[:, where], own.at[pair], refs.load_sem.at[pair])

    load(1 - core).start()
    load(core).start()
    ps_ref = refs.slots
    ps_load = pltpu.make_async_copy(ps_any, ps_ref, refs.ps_sem)
    ps_load.start()
    barrier = pltpu.get_barrier_semaphore()
    greet(sibling)
    greet(far)

    @pl.loop(1, XY)
    def _(step):
        greet(plane_peer(step))

    @pl.loop(1, 4)
    def _(step):
        greet(z_peer(step))

    routes = types.SimpleNamespace()
    raw_refs = types.SimpleNamespace(**{n[4:]: r for n, r in vars(refs).items() if n.startswith("raw_")})
    late_refs = types.SimpleNamespace(**{n[5:]: r for n, r in vars(refs).items() if n.startswith("late_")})
    raw_count = raw_rows // RAW_CHUNK
    late_count = (rows_here - raw_rows) // LATE_CHUNK
    def column(pair, half):
        return pl.ds(pl.multiple_of(pair * 2 * BW + half * BW, BW), BW)

    def put_raw(entry, rows, value):
        refs.raw_fin[entry, rows, :] = value

    def put_late(entry, rows, value):
        out_ref[rows, column(entry, 1)] = value

    raw = Stream(True, own, 0, raw_count, RAW_CHUNK, raw_refs, routes, put_raw, 0, place)
    late = Stream(False, refs.rights, 0, late_count, LATE_CHUNK, late_refs, routes, put_late, raw_rows, place)
    first_batch = RAW_FIRST[cap]
    first_sent = RAW_SENT[cap]

    def go_raw(forwards, backs):
        raw.go(first_batch + forwards * 2 // cap, first_batch + backs * 2 // cap)

    def go_late(forwards, backs):
        late.go(forwards * 2 // cap, backs * 2 // cap)

    def gram(pair, target):
        load(pair).wait()
        high, low = split(own[pair])
        xh[pair] = high
        xl[pair] = low
        rows = ((0,), (0,))
        cross = dot3((high[:, :BW], low[:, :BW]), (high[:, BW:], low[:, BW:]), rows)
        target[:, 0:16, :] = cross[:, :128].reshape(XY, 16, 128)
        target[:, 16:32, :] = cross[:, 128:].reshape(XY, 16, 128)
        values = own[pair]
        tile = row_of(jnp.sum(values * values, axis=0, keepdims=True))
        target[:, 32:40, :] = jnp.broadcast_to(tile[None], (XY, 8, 128))

    gmine, gsend, gpeer, rs = refs.gmine, refs.gsend, refs.gpeer, refs.rs
    gram(1 - core, gsend)
    gram(core, gmine)
    pl.semaphore_wait(barrier, 20)
    to_sibling = remote(gsend, gpeer, refs.pair_s, refs.pair_r, sibling)
    to_sibling.start()

    raw.send(0, first_sent)
    to_sibling.wait_recv()
    gmine[...] = gmine[...] + gpeer[...]

    def rs_copy(step):
        target = (xy + step) % XY
        return remote(gmine.at[target], rs.at[xy], refs.rs_s, refs.rs_r, plane_peer(step))

    def gather_copy(buffer, send, recv):
        return lambda step: remote(buffer.at[xy], buffer.at[xy], send, recv, plane_peer(step))

    def start_all(copy, last=XY):
        @pl.loop(1, last)
        def _(step):
            copy(step).start()

    def others(buffer, send, recv, device, last=XY):
        part = buffer.at[pl.ds(0, last - 1)]
        return remote(part, part, send, recv, device)

    start_all(rs_copy)
    rs[xy] = gmine[xy]

    ps_load.wait()
    vars(routes).update(vars(routes_of(ps_ref, side, cap)))
    raw.go(first_batch, 0)
    others(rs, refs.rs_s, refs.rs_r, plane_peer(1)).wait_recv()
    total = rs[0]
    for chip in range(1, XY):
        total = total + rs[chip]
    refs.zsend[...] = total
    to_far = remote(refs.zsend, refs.zrecv, refs.z_s, refs.z_r, far)
    to_far.start()
    raw.go(first_batch, RAW_BACK[cap])
    to_far.wait_recv()
    total = refs.zsend[...] + refs.zrecv[...]
    diag_tile = total[32:40, :]
    ag, zl, fp, fag = refs.ag, refs.zl, refs.fp, refs.fag
    ag[xy] = total[0:32, :]
    zl[z] = total
    ag_copy = gather_copy(ag, refs.ag_s, refs.ag_r)
    start_all(ag_copy)

    def zl_copy(step):
        return remote(zl.at[z], zl.at[z], refs.zl_s, refs.zl_r, z_peer(step))

    start_all(zl_copy, 4)
    raw.send(first_sent, raw_count)
    go_raw(2, 0)
    go_raw(3, 1)
    others(ag, refs.ag_s, refs.ag_r, plane_peer(1)).wait_recv()

    coupling, scale = coupling_of(ag[...], diag_tile)
    go_raw(4, 2)
    rsend, rrecv = refs.rsend, refs.rrecv
    rsend[0] = coupling
    to_sibling_k = remote(rsend.at[0], rrecv.at[0], refs.ro_s.at[2], refs.ro_r.at[2], sibling)
    to_sibling_k.start()
    coupling_parts = split(coupling)
    outer_product = dot3(coupling_parts, coupling_parts, ((1,), (1,)))
    inner_product = dot3(coupling_parts, coupling_parts, ((0,), (0,)))
    others(zl, refs.zl_s, refs.zl_r, z_peer(1), 4).wait_recv()
    fp[core] = zl[...]
    to_sibling_z = remote(zl, fp.at[core], refs.fp_s, refs.fp_r, sibling)
    to_sibling_z.start()
    fag_copy = gather_copy(fag, refs.fag_s, refs.fag_r)
    incoming_diag = []

    def gather_incoming():
        remote(zl, fp.at[1 - core], refs.fp_s, refs.fp_r, sibling).wait_recv()
        parity, plane = jnp.int32(0), jnp.int32(0)
        for pair in range(8):
            hit = ps_ref[pair] == 2 * z + core
            parity = jnp.where(hit, pair % 2, parity)
            plane = jnp.where(hit, pair // 2, plane)
        incoming = fp[parity, plane]
        fag[xy] = incoming[0:32, :]
        incoming_diag.append(incoming[32:40, :])
        start_all(fag_copy)

    def beside(sweep):
        go_raw(*((5, 3), (6, 3), (7, 4))[sweep])

    go_raw(5, 2)
    left_part, right_part = polynomials(
        [outer_product, inner_product], scale, beside
    )
    rsend[1] = right_part
    to_sibling_r = remote(rsend.at[1], rrecv.at[1], refs.ro_s.at[0], refs.ro_r.at[0], sibling)
    to_sibling_r.start()
    rsend[2] = left_part
    to_sibling_l = remote(rsend.at[2], rrecv.at[2], refs.ro_s.at[1], refs.ro_r.at[1], sibling)
    to_sibling_l.start()

    def spread(half, pair, blocks):
        for row_block, block in enumerate(blocks):
            high, low = split(block)
            where = (half, pair, pl.ds(row_block * BW, BW))
            rh[where] = high
            rl[where] = low

    rights = refs.rights
    esend, epeer, exy, ez = refs.esend, refs.epeer, refs.exy, refs.ez

    def rotate(half, pair, first, last):
        rows = pl.ds(first, last - first)
        result = dot3((xh[pair, rows, :], xl[pair, rows, :]), (rh[half, pair], rl[half, pair]))
        if half == 0:
            out_ref[rows, column(pair, 0)] = result
        elif first > 0:
            rights[pair] = result
        return jnp.sum(result * result, axis=0, keepdims=True)

    def across_of(source, entry):
        return dot3(split(source[0]), split(source[entry]))

    acrosses = [across_of(rsend, 1)]
    spread(1, core, (acrosses[0], right_part))
    right_sums = [rotate(1, core, raw_rows, rows_here)]
    late.send_slot(core, 0, EARLY)
    go_raw(9, 5)
    gather_incoming()
    go_raw(10, 6)
    to_sibling_k.wait_recv()
    to_sibling_r.wait_recv()
    acrosses.append(across_of(rrecv, 1))
    spread(1, 1 - core, (acrosses[1], rrecv[1]))
    right_sums.append(rotate(1, 1 - core, raw_rows, rows_here))

    late.send_slot(1 - core, 0, EARLY)
    late.send(EARLY, late_count)
    go_raw(raw_count, 7)
    to_sibling_l.wait_recv()
    left_sums = []

    def rotate_left(pair, source):
        spread(0, pair, (source[2], -jnp.transpose(acrosses[len(left_sums)])))
        left_sums.append(rotate(0, pair, 0, rows_here))

    rotate_left(core, rsend)
    go_raw(raw_count, 8)
    rotate_left(1 - core, rrecv)
    go_raw(raw_count, 9)
    go_late(1, 0)
    for entry, pair in enumerate((core, 1 - core)):
        sums = right_sums[entry] + rotate(1, pair, 0, raw_rows)
        esend[pair] = row_of(jnp.concatenate([left_sums[entry], sums], 1))
    e_sibling = remote(esend, epeer, refs.e_s.at[0], refs.e_r.at[0], sibling)
    e_sibling.start()
    go_raw(raw_count, 9)
    go_late(3, 0)
    raw.go(raw_count, raw_count)

    others(fag, refs.fag_s, refs.fag_r, plane_peer(1)).wait_recv()
    fsend, frecv, fh, fl = refs.fsend, refs.frecv, refs.fh, refs.fl
    coupling, scale = coupling_of(fag[...], incoming_diag[0])
    coupling_parts = split(coupling)
    go_late(5, 0)
    inner_product = dot3(coupling_parts, coupling_parts, ((0,), (0,)))
    e_sibling.wait_recv()
    exy[xy] = esend[...] + epeer[...]
    exy_copy = gather_copy(exy, refs.exy_s, refs.exy_r)
    start_all(exy_copy)
    go_late(8, 1)
    (right_part,) = polynomials(
        [inner_product], scale, lambda sweep: go_late(*((9, 2), (11, 3), (12, 5))[sweep])
    )
    fsend[1] = right_part
    fsend[0] = dot3(coupling_parts, split(right_part))
    to_sibling_f = remote(fsend, frecv, refs.f_s, refs.f_r, sibling)
    to_sibling_f.start()
    raw.arrivals()
    go_late(14, 7)
    others(exy, refs.exy_s, refs.exy_r, plane_peer(1)).wait_recv()
    plane_sum = exy[0]
    for chip in range(1, XY):
        plane_sum = plane_sum + exy[chip]
    ez[0] = plane_sum
    e_far = remote(ez.at[0], ez.at[1], refs.e_s.at[1], refs.e_r.at[1], far)
    e_far.start()

    def finish_raw(slot, source):
        for block in range(2):
            high, low = split(source[block])
            fh[slot, pl.ds(block * BW, BW), :] = high
            fl[slot, pl.ds(block * BW, BW), :] = low
        out_ref[pl.ds(0, raw_rows), column(slot, 1)] = dot3(split(refs.raw_fin[slot]), (fh[slot], fl[slot]))

    finish_raw(core, fsend)
    go_late(16, 9)
    to_sibling_f.wait_recv()
    finish_raw(1 - core, frecv)
    late.finish()
    late.arrivals()
    e_far.wait_recv()
    energies = (ez[0] + ez[1]) / (4 * XY * rows_here)
    en_ref[0:4, :] = energies[0, 0:4, :]
    en_ref[4:8, :] = energies[1, 0:4, :]

    for copy in (to_sibling, to_sibling_k, to_sibling_r, to_sibling_l, to_sibling_z, to_sibling_f, to_far, e_sibling, e_far):
        copy.wait_send()

    for buffer, send, recv in (
        (rs, refs.rs_s, refs.rs_r), (ag, refs.ag_s, refs.ag_r), (fag, refs.fag_s, refs.fag_r), (exy, refs.exy_s, refs.exy_r)
    ):
        others(buffer, send, recv, plane_peer(1)).wait_send()
    others(zl, refs.zl_s, refs.zl_r, z_peer(1), 4).wait_send()
    raw.drain()
    late.drain()


def call(cap, snapshots, partner_slot):
    rows = snapshots.shape[0]
    raw_rows = RAW_ROWS[cap]
    dma = pltpu.SemaphoreType.DMA
    f32 = lambda *shape: pltpu.VMEM(shape, F32)
    b16 = lambda *shape: pltpu.VMEM(shape, BF16)
    scratch = dict(
        own=f32(2, rows, 2 * BW), xh=b16(2, rows, 2 * BW), xl=b16(2, rows, 2 * BW),
        rh=b16(2, 2, 2 * BW, BW), rl=b16(2, 2, 2 * BW, BW),
        rights=f32(2, rows - raw_rows, BW),
        gmine=f32(XY, 40, 128), gsend=f32(XY, 40, 128), gpeer=f32(XY, 40, 128), rs=f32(XY, 40, 128),
        zsend=f32(40, 128), zrecv=f32(40, 128), ag=f32(XY, 32, 128),
        zl=f32(4, 40, 128), fp=f32(2, 4, 40, 128), fag=f32(XY, 32, 128),
        rsend=f32(3, BW, BW), rrecv=f32(3, BW, BW),
        fsend=f32(2, BW, BW), frecv=f32(2, BW, BW), fh=b16(2, 2 * BW, BW), fl=b16(2, 2 * BW, BW),
        esend=f32(2, 8, 128), epeer=f32(2, 8, 128), exy=f32(XY, 2, 8, 128), ez=f32(2, 2, 8, 128),
        slots=pltpu.SMEM((8,), jnp.int32), ps_sem=dma, load_sem=dma((2,)), pair_s=dma, pair_r=dma, rs_s=dma, rs_r=dma,
        z_s=dma, z_r=dma, ag_s=dma, ag_r=dma, zl_s=dma, zl_r=dma,
        fp_s=dma, fp_r=dma, fag_s=dma, fag_r=dma, ro_s=dma((3,)), ro_r=dma((3,)), f_s=dma, f_r=dma,
        e_s=dma((2,)), e_r=dma((2,)), exy_s=dma, exy_r=dma,
        raw_fin=f32(2, raw_rows, 2 * BW),
    )
    for name, height, width, chunk in (
        ("raw", raw_rows, 2 * BW, RAW_CHUNK), ("late", rows - raw_rows, BW, LATE_CHUNK)
    ):
        for buffer, blocks in (("mid_stage", cap), ("from_mid", cap), ("out_stage", 2), ("from_outer", 2), ("from_inner", 2)):
            scratch[f"{name}_{buffer}"] = f32(blocks, height, width)
        for sem in ("in_s", "mid_s", "out_s"):
            scratch[f"{name}_{sem}"] = dma
        for sem in ("in_r", "mid_r", "out_r"):
            scratch[f"{name}_{sem}"] = dma((height // chunk,))
    scratch["raw_out_r"] = dma
    return pl.pallas_call(
        functools.partial(kernel, cap, tuple(scratch)),
        out_shape=(
            jax.ShapeDtypeStruct(snapshots.shape, F32),
            jax.ShapeDtypeStruct((8, 128), F32),
        ),
        in_specs=[pl.BlockSpec(memory_space=pl.ANY)] * 2,
        out_specs=(pl.BlockSpec(memory_space=pltpu.VMEM), pl.BlockSpec(memory_space=pltpu.VMEM)),
        scratch_shapes=list(scratch.values()),
        name=f"round_{cap}",
        compiler_params=pltpu.CompilerParams(
            collective_id=cap, has_side_effects=True, vmem_limit_bytes=48 << 20
        ),
    )(snapshots, partner_slot)


def hand_out(moved_ref, energies_ref, out_ref, en_ref, sems):
    rows = moved_ref.shape[0] // 4
    copies = [pltpu.make_async_copy(energies_ref, en_ref, sems.at[4])]
    for part in range(4):
        where = pl.ds(part * rows, rows)
        copies.append(pltpu.make_async_copy(moved_ref.at[where], out_ref.at[where], sems.at[part]))
    for copy in copies:
        copy.start()
    for copy in copies:
        copy.wait()


def on_device(snapshots, partner_slot):
    crossing = jnp.sum((partner_slot[:4] >= 4).astype(jnp.int32))
    moved, energies = lax.switch(
        jnp.maximum(crossing, 2) - 2,
        [functools.partial(call, cap) for cap in (2, 3, 4)],
        snapshots,
        partner_slot,
    )
    anywhere = pl.BlockSpec(memory_space=pl.ANY)
    moved, energies = pl.pallas_call(
        hand_out,
        out_shape=(
            jax.ShapeDtypeStruct(moved.shape, F32),
            jax.ShapeDtypeStruct(energies.shape, F32),
        ),
        in_specs=[anywhere, anywhere],
        out_specs=(anywhere, anywhere),
        scratch_shapes=[pltpu.SemaphoreType.DMA((5,))],
        name="hand_out",
    )(moved, energies)
    return moved, energies.reshape(-1)


def solution(mesh):
    in_specs = (P("rows", "cols"), P())
    out_specs = (P("rows", "cols"), P("cols"))
    return jax.shard_map(
        on_device, mesh=mesh, in_specs=in_specs, out_specs=out_specs, check_vma=False
    )
```

```python
import functools
import types

import jax
import jax.numpy as jnp
from jax import lax
from jax.experimental import pallas as pl
from jax.experimental.pallas import tpu as pltpu
from jax.sharding import PartitionSpec as P

BW = 256
SWEEPS = 4
MESH = pl.DeviceIdType.MESH
F32 = jnp.float32
BF16 = jnp.bfloat16
XY = 16
RAW_CHUNK = 16
LATE_CHUNK = 16
EARLY = 6
RAW_FIRST = {2: 4, 3: 3, 4: 2}
RAW_SENT = {2: 7, 3: 5, 4: 4}
RAW_ROWS = {2: 208, 3: 144, 4: 128}


def split(value):
    high = value.astype(BF16)
    return high, (value - high.astype(F32)).astype(BF16)


def dot(left, right, contract=((1,), (0,))):
    return lax.dot_general(left, right, (contract, ((), ())), preferred_element_type=F32)


def dot3(left, right, contract=((1,), (0,))):
    return dot(left[0], right[0], contract) + (
        dot(left[0], right[1], contract) + dot(left[1], right[0], contract)
    )


def coupling_of(pieces, diag_tile):
    cross = jnp.concatenate(
        [pieces[:, 0:16, :].reshape(BW, 128), pieces[:, 16:32, :].reshape(BW, 128)], 1
    )
    left_cols = []
    right_rows = []
    for half in range(2):
        left_row = jnp.broadcast_to(diag_tile[half : half + 1, :], (128, 128))
        left_cols.append(jnp.transpose(left_row))
        right_rows.append(diag_tile[2 + half : 3 + half, :])
    left = jnp.concatenate([jnp.concatenate([part, part], 1) for part in left_cols], 0)
    right = jnp.broadcast_to(jnp.concatenate(right_rows, 1), (BW, BW))
    gap = right - left
    coupling = cross * gap / (gap * gap + 4.0 * cross * cross + 0.25 * left * right)
    scale = lax.rsqrt(jnp.full((1, 1), 1.0, F32) + 2.0 * jnp.sum(coupling * coupling))
    return coupling, scale


def polynomials(starts, scale, between):
    eye = (
        lax.broadcasted_iota(jnp.int32, (BW, BW), 0) == lax.broadcasted_iota(jnp.int32, (BW, BW), 1)
    ).astype(F32)

    def times(uppers, lowers, rights):
        stacks = [jnp.concatenate(parts, 0) for parts in zip(uppers, lowers)]
        results = [dot3(split(stack), split(right)) for stack, right in zip(stacks, rights)]
        return [result[:BW] for result in results], [result[BW:] for result in results]

    firsts = [(eye + start) * (scale * scale) for start in starts]
    parts = [split(first) for first in firsts]
    powers = [dot3(part, part) for part in parts]
    squares, crossed = times(
        [0.25 * first - 1.5 * eye for first in firsts],
        [1.125 * first - 0.125 * power for first, power in zip(firsts, powers)],
        powers,
    )
    squares = [square + 2.25 * first for square, first in zip(squares, firsts)]
    totals = [
        scale * (2.25 * eye - 2.4375 * first + 1.6875 * power - 0.5 * cross)
        for first, power, cross in zip(firsts, powers, crossed)
    ]
    for sweep in range(2, SWEEPS):
        between(2 * sweep - 4)
        powers, crossed = times(squares, totals, squares)
        factors = [2.25 * eye - 1.5 * square + 0.25 * power for square, power in zip(squares, powers)]
        if sweep < SWEEPS - 1:
            between(1)
            squares, crossed = times(squares, crossed, factors)
        else:
            crossed = [dot3(split(cross), split(factor)) for cross, factor in zip(crossed, factors)]
        totals = [1.5 * total - 0.5 * cross for total, cross in zip(totals, crossed)]
    return totals


def pick(options, index):
    value = options[0]
    for position in range(1, len(options)):
        value = jnp.where(index == position, options[position], value)
    return value


def remote(src, dst, send, recv, device):
    return pltpu.make_async_remote_copy(
        src_ref=src, dst_ref=dst, send_sem=send, recv_sem=recv, device_id=device, device_id_type=MESH
    )


def row_of(values):
    return jnp.concatenate(
        [values[:, 128 * part : 128 * (part + 1)] for part in range(4)] + [jnp.zeros((4, 128), F32)], 0
    )


class Stream:
    def __init__(self, whole, near, first, count, chunk, refs, routes, put, fin_first, place):
        self.whole = whole
        self.forwards = self.backs = 0
        self.near, self.first, self.count, self.chunk, self.refs = near, first, count, chunk, refs
        self.routes, self.put, self.fin_first, self.place = routes, put, fin_first, place

    def rows(self, index, offset=0):
        return pl.ds(pl.multiple_of(offset + index * self.chunk, self.chunk), self.chunk)

    def near_rows(self, index):
        return self.rows(index, self.first)

    def in_copy(self, index, device):
        refs = self.refs
        return remote(
            self.near.at[:, self.near_rows(index)], refs.from_outer.at[:, self.rows(index)],
            refs.in_s, refs.in_r.at[index], device,
        )

    def mid_copy(self, index):
        refs = self.refs
        return remote(
            refs.mid_stage.at[:, self.rows(index)], refs.from_mid.at[:, self.rows(index)],
            refs.mid_s, refs.mid_r.at[index], self.place.mid_peer,
        )

    def out_copy(self, index, device):
        refs = self.refs
        return remote(
            refs.out_stage.at[:, self.rows(index)], refs.from_inner.at[:, self.rows(index)],
            refs.out_s, self.out_sem(index), device,
        )

    def out_sem(self, index):
        return self.refs.out_r if self.whole else self.refs.out_r.at[index]

    def near_options(self, index):
        return [self.near[entry, self.near_rows(index), :] for entry in range(2)]

    def forward(self, index):
        self.in_copy(index, self.place.outer_peer).wait_recv()
        rows = self.rows(index)
        refs = self.refs
        options = self.near_options(index) + [refs.from_outer[entry, rows, :] for entry in range(2)]
        for entry in range(refs.mid_stage.shape[0]):
            refs.mid_stage[entry, rows, :] = pick(options, self.routes.mid[entry])
        self.mid_copy(index).start()

    def back(self, index):
        self.mid_copy(index).wait_recv()
        rows = self.rows(index)
        refs = self.refs
        near = self.near_options(index)
        beyond = [refs.from_mid[entry, rows, :] for entry in range(refs.from_mid.shape[0])]
        for entry in range(2):
            refs.out_stage[entry, rows, :] = pick(near + beyond, self.routes.out[entry])
        self.out_copy(index, self.place.outer_peer).start()
        options = near + [refs.from_outer[entry, rows, :] for entry in range(2)] + beyond
        for entry in range(2):
            self.put(entry, self.rows(index, self.fin_first), pick(options, self.routes.inner[entry]))

    def arrive(self, index):
        if not self.whole:
            self.out_copy(index, self.place.inner_peer).wait_recv()
        rows = self.rows(index)
        options = self.near_options(index) + [self.refs.from_inner[entry, rows, :] for entry in range(2)]
        for entry in range(2):
            self.put(entry, self.rows(index, self.fin_first), pick(options, self.routes.outer[entry]))

    def send(self, first, last):
        @pl.when(self.place.is_outer)
        def _():
            @pl.loop(first, last)
            def _(index):
                self.in_copy(index, self.place.inner_peer).start()

    def send_slot(self, slot, first, last):
        refs = self.refs

        @pl.when(self.place.is_outer)
        def _():
            @pl.loop(first, last)
            def _(index):
                remote(
                    self.near.at[slot, self.near_rows(index)], refs.from_outer.at[slot, self.rows(index)],
                    refs.in_s, refs.in_r.at[index], self.place.inner_peer,
                ).start()

    def go(self, forwards, backs):
        forwards = max(self.forwards, min(forwards, self.count))
        backs = max(self.backs, min(backs, forwards))

        @pl.when(self.place.is_inner)
        def _():
            pl.loop(self.forwards, forwards)(self.forward)
            pl.loop(self.backs, backs)(self.back)

        self.forwards, self.backs = forwards, backs

    def finish(self):
        ahead = self.forwards - self.backs
        first, last = self.backs, self.count - ahead

        @pl.when(self.place.is_inner)
        def _():
            @pl.loop(first, last)
            def _(index):
                self.back(index)
                self.forward(index + ahead)

        self.forwards, self.backs = self.count, last
        self.go(self.count, self.count)

    def arrivals(self):
        @pl.when(self.place.is_outer)
        def _():
            if self.whole:
                refs = self.refs
                remote(
                    refs.out_stage, refs.from_inner, refs.out_s, refs.out_r, self.place.inner_peer
                ).wait_recv()
            pl.loop(0, self.count)(self.arrive)

    def drain(self):
        refs, place = self.refs, self.place

        @pl.when(place.is_outer)
        def _():
            sent = self.near.at[:, pl.ds(self.first, self.count * self.chunk)]
            remote(sent, refs.from_outer, refs.in_s, refs.in_r.at[0], place.inner_peer).wait_send()

        @pl.when(place.is_inner)
        def _():
            remote(refs.mid_stage, refs.from_mid, refs.mid_s, refs.mid_r.at[0], place.mid_peer).wait_send()
            remote(
                refs.out_stage, refs.from_inner, refs.out_s, self.out_sem(0), place.outer_peer
            ).wait_send()


def routes_of(ps_ref, side, cap):
    slots = []
    for first, second in zip((2, 3, 0, 1, 4, 5, 6, 7), (4, 5, 6, 7, 2, 3, 0, 1)):
        slot = ps_ref[first + side * (second - first)]
        low_side = jnp.where(slot < 2, slot + 2, jnp.where(slot < 4, slot - 2, slot))
        high_side = jnp.where(slot < 2, slot + 6, jnp.where(slot < 4, slot + 2, slot - 4))
        slots.append(jnp.where(side == 0, low_side, high_side))
    crosses = lambda slot: slot >= 4
    returns = lambda slot: slot < 4
    outward = lambda slot: (slot == 2) | (slot == 3)

    def ranks(order, wanted):
        count = jnp.int32(0)
        result = {}
        for position in order:
            result[position] = count
            count = count + jnp.where(wanted(slots[position]), 1, 0)
        return result

    def source_of(places, wanted):
        found = jnp.int32(0)
        for position, place in places.items():
            found = jnp.where(wanted(position), place, found)
        return found

    send_rank = ranks((0, 1, 2, 3), crosses)
    recv_rank = ranks((4, 5, 6, 7), returns)
    out_rank = ranks((0, 1, 4, 5, 6, 7), outward)
    far_places = {position: recv_rank[position] for position in (4, 5, 6, 7)}
    mid_places = {position: position for position in range(4)}
    out_places = {0: 0, 1: 1, **{position: 2 + place for position, place in far_places.items()}}
    inner_places = {**mid_places, **{position: 4 + place for position, place in far_places.items()}}
    outer_places = {2: 0, 3: 1, **{position: 2 + rank for position, rank in out_rank.items()}}
    return types.SimpleNamespace(
        mid=[
            source_of(mid_places, lambda p: crosses(slots[p]) & (send_rank[p] == entry))
            for entry in range(cap)
        ],
        out=[
            source_of(out_places, lambda p: outward(slots[p]) & (out_rank[p] == entry))
            for entry in range(2)
        ],
        inner=[source_of(inner_places, lambda p: slots[p] == entry) for entry in range(2)],
        outer=[source_of(outer_places, lambda p: slots[p] == 2 + entry) for entry in range(2)],
    )


def kernel(cap, names, x_hbm, ps_any, out_ref, en_ref, *scratch):
    refs = types.SimpleNamespace(**dict(zip(names, scratch)))
    own, xh, xl, rh, rl = refs.own, refs.xh, refs.xl, refs.rh, refs.rl
    rows_here = own.shape[1]
    raw_rows = refs.raw_fin.shape[1]
    row = lax.axis_index("rows")
    z = lax.axis_index("cols")
    core = row % 2
    xy = (row // 2) % XY
    zh = row // (2 * XY)
    side = z // 2
    place = types.SimpleNamespace(
        is_outer=(z % 3) == 0,
        is_inner=(z % 3) != 0,
        inner_peer={"cols": 1 + z // 3},
        outer_peer={"cols": (3 * z + 1) % 4},
        mid_peer={"cols": 3 - z},
    )
    sibling = {"rows": row + 1 - 2 * core}
    far = {"rows": (row + 2 * XY) % (4 * XY)}

    def plane_peer(step):
        return {"rows": zh * 2 * XY + ((xy + step) % XY) * 2 + core}

    def z_peer(step):
        return {"cols": (z + step) % 4}

    def greet(device):
        pl.semaphore_signal(barrier, inc=1, device_id=device, device_id_type=MESH)

    def load(pair):
        where = pl.ds(pl.multiple_of(pair * 2 * BW, 2 * BW), 2 * BW)
        return pltpu.make_async_copy(x_hbm.at[:, where], own.at[pair], refs.load_sem.at[pair])

    load(1 - core).start()
    load(core).start()
    ps_ref = refs.slots
    ps_load = pltpu.make_async_copy(ps_any, ps_ref, refs.ps_sem)
    ps_load.start()
    barrier = pltpu.get_barrier_semaphore()
    greet(sibling)
    greet(far)

    @pl.loop(1, XY)
    def _(step):
        greet(plane_peer(step))

    @pl.loop(1, 4)
    def _(step):
        greet(z_peer(step))

    routes = types.SimpleNamespace()
    raw_refs = types.SimpleNamespace(**{n[4:]: r for n, r in vars(refs).items() if n.startswith("raw_")})
    late_refs = types.SimpleNamespace(**{n[5:]: r for n, r in vars(refs).items() if n.startswith("late_")})
    raw_count = raw_rows // RAW_CHUNK
    late_count = (rows_here - raw_rows) // LATE_CHUNK
    def column(pair, half):
        return pl.ds(pl.multiple_of(pair * 2 * BW + half * BW, BW), BW)

    def put_raw(entry, rows, value):
        refs.raw_fin[entry, rows, :] = value

    def put_late(entry, rows, value):
        out_ref[rows, column(entry, 1)] = value

    raw = Stream(True, own, 0, raw_count, RAW_CHUNK, raw_refs, routes, put_raw, 0, place)
    late = Stream(False, refs.rights, 0, late_count, LATE_CHUNK, late_refs, routes, put_late, raw_rows, place)
    first_batch = RAW_FIRST[cap]
    first_sent = RAW_SENT[cap]

    def go_raw(forwards, backs):
        raw.go(first_batch + forwards * 2 // cap, first_batch + backs * 2 // cap)

    def go_late(forwards, backs):
        late.go(forwards * 2 // cap, backs * 2 // cap)

    def gram(pair, target):
        load(pair).wait()
        high, low = split(own[pair])
        xh[pair] = high
        xl[pair] = low
        rows = ((0,), (0,))
        cross = dot3((high[:, :BW], low[:, :BW]), (high[:, BW:], low[:, BW:]), rows)
        target[:, 0:16, :] = cross[:, :128].reshape(XY, 16, 128)
        target[:, 16:32, :] = cross[:, 128:].reshape(XY, 16, 128)
        values = own[pair]
        tile = row_of(jnp.sum(values * values, axis=0, keepdims=True))
        target[:, 32:40, :] = jnp.broadcast_to(tile[None], (XY, 8, 128))

    gmine, gsend, gpeer, rs = refs.gmine, refs.gsend, refs.gpeer, refs.rs
    gram(1 - core, gsend)
    gram(core, gmine)
    pl.semaphore_wait(barrier, 20)
    to_sibling = remote(gsend, gpeer, refs.pair_s, refs.pair_r, sibling)
    to_sibling.start()

    raw.send(0, first_sent)
    to_sibling.wait_recv()
    gmine[...] = gmine[...] + gpeer[...]

    def rs_copy(step):
        target = (xy + step) % XY
        return remote(gmine.at[target], rs.at[xy], refs.rs_s, refs.rs_r, plane_peer(step))

    def gather_copy(buffer, send, recv):
        return lambda step: remote(buffer.at[xy], buffer.at[xy], send, recv, plane_peer(step))

    def start_all(copy, last=XY):
        @pl.loop(1, last)
        def _(step):
            copy(step).start()

    def others(buffer, send, recv, device, last=XY):
        part = buffer.at[pl.ds(0, last - 1)]
        return remote(part, part, send, recv, device)

    start_all(rs_copy)
    rs[xy] = gmine[xy]

    ps_load.wait()
    vars(routes).update(vars(routes_of(ps_ref, side, cap)))
    raw.go(first_batch, 0)
    others(rs, refs.rs_s, refs.rs_r, plane_peer(1)).wait_recv()
    total = rs[0]
    for chip in range(1, XY):
        total = total + rs[chip]
    refs.zsend[...] = total
    to_far = remote(refs.zsend, refs.zrecv, refs.z_s, refs.z_r, far)
    to_far.start()
    to_far.wait_recv()
    total = refs.zsend[...] + refs.zrecv[...]
    diag_tile = total[32:40, :]
    ag, zl, fp, fag = refs.ag, refs.zl, refs.fp, refs.fag
    ag[xy] = total[0:32, :]
    zl[z] = total
    ag_copy = gather_copy(ag, refs.ag_s, refs.ag_r)
    start_all(ag_copy)

    def zl_copy(step):
        return remote(zl.at[z], zl.at[z], refs.zl_s, refs.zl_r, z_peer(step))

    start_all(zl_copy, 4)
    raw.send(first_sent, raw_count)
    go_raw(2, 0)
    go_raw(3, 1)
    others(ag, refs.ag_s, refs.ag_r, plane_peer(1)).wait_recv()

    coupling, scale = coupling_of(ag[...], diag_tile)
    go_raw(4, 2)
    rsend, rrecv = refs.rsend, refs.rrecv
    rsend[0] = coupling
    to_sibling_k = remote(rsend.at[0], rrecv.at[0], refs.ro_s.at[2], refs.ro_r.at[2], sibling)
    to_sibling_k.start()
    coupling_parts = split(coupling)
    outer_product = dot3(coupling_parts, coupling_parts, ((1,), (1,)))
    inner_product = dot3(coupling_parts, coupling_parts, ((0,), (0,)))
    others(zl, refs.zl_s, refs.zl_r, z_peer(1), 4).wait_recv()
    fp[core] = zl[...]
    to_sibling_z = remote(zl, fp.at[core], refs.fp_s, refs.fp_r, sibling)
    to_sibling_z.start()
    fag_copy = gather_copy(fag, refs.fag_s, refs.fag_r)
    incoming_diag = []

    def gather_incoming():
        remote(zl, fp.at[1 - core], refs.fp_s, refs.fp_r, sibling).wait_recv()
        parity, plane = jnp.int32(0), jnp.int32(0)
        for pair in range(8):
            hit = ps_ref[pair] == 2 * z + core
            parity = jnp.where(hit, pair % 2, parity)
            plane = jnp.where(hit, pair // 2, plane)
        incoming = fp[parity, plane]
        fag[xy] = incoming[0:32, :]
        incoming_diag.append(incoming[32:40, :])
        start_all(fag_copy)

    def beside(sweep):
        go_raw(*((5, 3), (6, 3), (7, 4))[sweep])

    go_raw(5, 2)
    left_part, right_part = polynomials(
        [outer_product, inner_product], scale, beside
    )
    rsend[1] = right_part
    to_sibling_r = remote(rsend.at[1], rrecv.at[1], refs.ro_s.at[0], refs.ro_r.at[0], sibling)
    to_sibling_r.start()
    rsend[2] = left_part
    to_sibling_l = remote(rsend.at[2], rrecv.at[2], refs.ro_s.at[1], refs.ro_r.at[1], sibling)
    to_sibling_l.start()

    def spread(half, pair, blocks):
        for row_block, block in enumerate(blocks):
            high, low = split(block)
            where = (half, pair, pl.ds(row_block * BW, BW))
            rh[where] = high
            rl[where] = low

    rights = refs.rights
    esend, epeer, exy, ez = refs.esend, refs.epeer, refs.exy, refs.ez

    def rotate(half, pair, first, last):
        rows = pl.ds(first, last - first)
        result = dot3((xh[pair, rows, :], xl[pair, rows, :]), (rh[half, pair], rl[half, pair]))
        if half == 0:
            out_ref[rows, column(pair, 0)] = result
        elif first > 0:
            rights[pair] = result
            return None
        return jnp.sum(result * result, axis=0, keepdims=True)

    def across_of(source, entry):
        return dot3(split(source[0]), split(source[entry]))

    acrosses = [across_of(rsend, 1)]
    spread(1, core, (acrosses[0], right_part))
    rotate(1, core, raw_rows, rows_here)
    late.send_slot(core, 0, EARLY)
    go_raw(9, 5)
    gather_incoming()
    go_raw(10, 6)
    to_sibling_k.wait_recv()
    to_sibling_r.wait_recv()
    acrosses.append(across_of(rrecv, 1))
    spread(1, 1 - core, (acrosses[1], rrecv[1]))
    rotate(1, 1 - core, raw_rows, rows_here)

    late.send_slot(1 - core, 0, EARLY)
    late.send(EARLY, late_count)
    go_raw(raw_count, 7)
    to_sibling_l.wait_recv()
    left_sums = []

    def rotate_left(pair, source):
        spread(0, pair, (source[2], -jnp.transpose(acrosses[len(left_sums)])))
        left_sums.append(rotate(0, pair, 0, rows_here))

    rotate_left(core, rsend)
    go_raw(raw_count, 8)
    rotate_left(1 - core, rrecv)
    go_raw(raw_count, 9)
    go_late(1, 0)
    for entry, pair in enumerate((core, 1 - core)):
        late_part = rights[pair]
        sums = jnp.sum(late_part * late_part, axis=0, keepdims=True) + rotate(1, pair, 0, raw_rows)
        esend[pair] = row_of(jnp.concatenate([left_sums[entry], sums], 1))
    e_sibling = remote(esend, epeer, refs.e_s.at[0], refs.e_r.at[0], sibling)
    e_sibling.start()
    go_raw(raw_count, 9)
    go_late(3, 0)
    raw.go(raw_count, raw_count)

    others(fag, refs.fag_s, refs.fag_r, plane_peer(1)).wait_recv()
    fsend, frecv, fh, fl = refs.fsend, refs.frecv, refs.fh, refs.fl
    coupling, scale = coupling_of(fag[...], incoming_diag[0])
    coupling_parts = split(coupling)
    go_late(5, 0)
    inner_product = dot3(coupling_parts, coupling_parts, ((0,), (0,)))
    e_sibling.wait_recv()
    exy[xy] = esend[...] + epeer[...]
    exy_copy = gather_copy(exy, refs.exy_s, refs.exy_r)
    start_all(exy_copy)
    go_late(8, 1)
    (right_part,) = polynomials(
        [inner_product], scale, lambda sweep: go_late(*((9, 2), (11, 3), (12, 5))[sweep])
    )
    fsend[1] = right_part
    fsend[0] = dot3(coupling_parts, split(right_part))
    to_sibling_f = remote(fsend, frecv, refs.f_s, refs.f_r, sibling)
    to_sibling_f.start()
    raw.arrivals()
    go_late(14, 7)
    others(exy, refs.exy_s, refs.exy_r, plane_peer(1)).wait_recv()
    plane_sum = exy[0]
    for chip in range(1, XY):
        plane_sum = plane_sum + exy[chip]
    ez[0] = plane_sum
    e_far = remote(ez.at[0], ez.at[1], refs.e_s.at[1], refs.e_r.at[1], far)
    e_far.start()

    def finish_raw(slot, source):
        for block in range(2):
            high, low = split(source[block])
            fh[slot, pl.ds(block * BW, BW), :] = high
            fl[slot, pl.ds(block * BW, BW), :] = low
        out_ref[pl.ds(0, raw_rows), column(slot, 1)] = dot3(split(refs.raw_fin[slot]), (fh[slot], fl[slot]))

    finish_raw(core, fsend)
    go_late(16, 9)
    to_sibling_f.wait_recv()
    finish_raw(1 - core, frecv)
    late.finish()
    late.arrivals()
    e_far.wait_recv()
    energies = (ez[0] + ez[1]) / (4 * XY * rows_here)
    en_ref[0:4, :] = energies[0, 0:4, :]
    en_ref[4:8, :] = energies[1, 0:4, :]

    for copy in (to_sibling, to_sibling_k, to_sibling_r, to_sibling_l, to_sibling_z, to_sibling_f, to_far, e_sibling, e_far):
        copy.wait_send()

    for buffer, send, recv in (
        (rs, refs.rs_s, refs.rs_r), (ag, refs.ag_s, refs.ag_r), (fag, refs.fag_s, refs.fag_r), (exy, refs.exy_s, refs.exy_r)
    ):
        others(buffer, send, recv, plane_peer(1)).wait_send()
    others(zl, refs.zl_s, refs.zl_r, z_peer(1), 4).wait_send()
    raw.drain()
    late.drain()


def call(cap, snapshots, partner_slot):
    rows = snapshots.shape[0]
    raw_rows = RAW_ROWS[cap]
    dma = pltpu.SemaphoreType.DMA
    f32 = lambda *shape: pltpu.VMEM(shape, F32)
    b16 = lambda *shape: pltpu.VMEM(shape, BF16)
    scratch = dict(
        own=f32(2, rows, 2 * BW), xh=b16(2, rows, 2 * BW), xl=b16(2, rows, 2 * BW),
        rh=b16(2, 2, 2 * BW, BW), rl=b16(2, 2, 2 * BW, BW),
        rights=f32(2, rows - raw_rows, BW),
        gmine=f32(XY, 40, 128), gsend=f32(XY, 40, 128), gpeer=f32(XY, 40, 128), rs=f32(XY, 40, 128),
        zsend=f32(40, 128), zrecv=f32(40, 128), ag=f32(XY, 32, 128),
        zl=f32(4, 40, 128), fp=f32(2, 4, 40, 128), fag=f32(XY, 32, 128),
        rsend=f32(3, BW, BW), rrecv=f32(3, BW, BW),
        fsend=f32(2, BW, BW), frecv=f32(2, BW, BW), fh=b16(2, 2 * BW, BW), fl=b16(2, 2 * BW, BW),
        esend=f32(2, 8, 128), epeer=f32(2, 8, 128), exy=f32(XY, 2, 8, 128), ez=f32(2, 2, 8, 128),
        slots=pltpu.SMEM((8,), jnp.int32), ps_sem=dma, load_sem=dma((2,)), pair_s=dma, pair_r=dma, rs_s=dma, rs_r=dma,
        z_s=dma, z_r=dma, ag_s=dma, ag_r=dma, zl_s=dma, zl_r=dma,
        fp_s=dma, fp_r=dma, fag_s=dma, fag_r=dma, ro_s=dma((3,)), ro_r=dma((3,)), f_s=dma, f_r=dma,
        e_s=dma((2,)), e_r=dma((2,)), exy_s=dma, exy_r=dma,
        raw_fin=f32(2, raw_rows, 2 * BW),
    )
    for name, height, width, chunk in (
        ("raw", raw_rows, 2 * BW, RAW_CHUNK), ("late", rows - raw_rows, BW, LATE_CHUNK)
    ):
        for buffer, blocks in (("mid_stage", cap), ("from_mid", cap), ("out_stage", 2), ("from_outer", 2), ("from_inner", 2)):
            scratch[f"{name}_{buffer}"] = f32(blocks, height, width)
        for sem in ("in_s", "mid_s", "out_s"):
            scratch[f"{name}_{sem}"] = dma
        for sem in ("in_r", "mid_r", "out_r"):
            scratch[f"{name}_{sem}"] = dma((height // chunk,))
    scratch["raw_out_r"] = dma
    return pl.pallas_call(
        functools.partial(kernel, cap, tuple(scratch)),
        out_shape=(
            jax.ShapeDtypeStruct(snapshots.shape, F32),
            jax.ShapeDtypeStruct((8, 128), F32),
        ),
        in_specs=[pl.BlockSpec(memory_space=pl.ANY)] * 2,
        out_specs=(pl.BlockSpec(memory_space=pltpu.VMEM), pl.BlockSpec(memory_space=pltpu.VMEM)),
        scratch_shapes=list(scratch.values()),
        name=f"round_{cap}",
        compiler_params=pltpu.CompilerParams(
            collective_id=cap, has_side_effects=True, vmem_limit_bytes=48 << 20
        ),
    )(snapshots, partner_slot)


def hand_out(moved_ref, energies_ref, out_ref, en_ref, sems):
    rows = moved_ref.shape[0] // 4
    copies = [pltpu.make_async_copy(energies_ref, en_ref, sems.at[4])]
    for part in range(4):
        where = pl.ds(part * rows, rows)
        copies.append(pltpu.make_async_copy(moved_ref.at[where], out_ref.at[where], sems.at[part]))
    for copy in copies:
        copy.start()
    for copy in copies:
        copy.wait()


def choose(ps_ref, branch_ref):
    crossing = jnp.int32(0)
    for pair in range(4):
        crossing = crossing + jnp.where(ps_ref[pair] >= 4, 1, 0)
    branch_ref[0] = jnp.maximum(crossing, 2) - 2


def on_device(snapshots, partner_slot):
    branch = pl.pallas_call(
        choose,
        out_shape=jax.ShapeDtypeStruct((1,), jnp.int32),
        in_specs=[pl.BlockSpec(memory_space=pltpu.SMEM)],
        out_specs=pl.BlockSpec(memory_space=pltpu.SMEM),
        name="choose",
    )(partner_slot)
    moved, energies = lax.switch(
        branch[0],
        [functools.partial(call, cap) for cap in (2, 3, 4)],
        snapshots,
        partner_slot,
    )
    anywhere = pl.BlockSpec(memory_space=pl.ANY)
    moved, energies = pl.pallas_call(
        hand_out,
        out_shape=(
            jax.ShapeDtypeStruct(moved.shape, F32),
            jax.ShapeDtypeStruct(energies.shape, F32),
        ),
        in_specs=[anywhere, anywhere],
        out_specs=(anywhere, anywhere),
        scratch_shapes=[pltpu.SemaphoreType.DMA((5,))],
        name="hand_out",
    )(moved, energies)
    return moved, energies.reshape(-1)


def solution(mesh):
    in_specs = (P("rows", "cols"), P())
    out_specs = (P("rows", "cols"), P("cols"))
    return jax.shard_map(
        on_device, mesh=mesh, in_specs=in_specs, out_specs=out_specs, check_vma=False
    )
```
